32 devices in a mesh: rep: 2 (over y), exp: 16 (over z, x, core).
Axes of the slice: x: 2, y: 2, z: 4, core: 2. Of those that a mesh axis runs over, the one named last changes fastest.
Arguments:
- tokens: bfloat16 [2, 768, 2048], P(None, ('rep', 'exp')), may hold values from -6 to 6
- cotangent: bfloat16 [2, 768, 2048], P(None, ('rep', 'exp')), may hold values from -12 to 12
- routes: int32 [2, 768, 8], P(None, ('rep', 'exp')), may hold values from 0 to 15, all different within a row; in each aligned block of 24 rows (0 to 23, 24 to 47, ..., all dimensions but the last counted through in order) at most 16 rows name the same one
- gates: bfloat16 [2, 768, 8], P(None, ('rep', 'exp')), may hold values from 0.049804688 to 0.34960938
- collapsed: int32 [16], P('exp'), may hold values 0 or 1
- w_in: bfloat16 [16, 2048, 1536], P('exp', 'rep'), may hold values from -5 to 5
- w_out: bfloat16 [16, 768, 2048], P('exp', 'rep'), may hold values from -5 to 5
- first_in: bfloat16 [16, 2048, 1536], P('exp', 'rep'), may hold values from -2 to 2
- second_in: bfloat16 [16, 2048, 1536], P('exp', 'rep'), may hold values from 0.0099487305 to 1
- first_out: bfloat16 [16, 768, 2048], P('exp', 'rep'), may hold values from -2 to 2
- second_out: bfloat16 [16, 768, 2048], P('exp', 'rep'), may hold values from 0.0099487305 to 1
- fresh_in: bfloat16 [16, 2048, 1536], P('exp', 'rep'), may hold values from -5 to 5
- fresh_out: bfloat16 [16, 768, 2048], P('exp', 'rep'), may hold values from -5 to 5
Outputs:
- d_tokens: bfloat16 [2, 768, 2048], P(None, ('rep', 'exp'))
- d_gates: bfloat16 [2, 768, 8], P(None, ('rep', 'exp'))
- new_w_in: bfloat16 [16, 2048, 1536], P('exp', 'rep')
- new_w_out: bfloat16 [16, 768, 2048], P('exp', 'rep')
- new_first_in: bfloat16 [16, 2048, 1536], P('exp', 'rep')
- new_second_in: bfloat16 [16, 2048, 1536], P('exp', 'rep')
- new_first_out: bfloat16 [16, 768, 2048], P('exp', 'rep')
- new_second_out: bfloat16 [16, 768, 2048], P('exp', 'rep')
The draws below stay inside these ranges and needn't reach their ends.
Inputs may be any that keep to these rules, and one draw needn't show every extreme that they name: `routes`: in each microbatch the 24 tokens of one device name no expert more than 16 times, and some device names some expert exactly 16 times; a token names 8 different experts.
All inputs are finite; a program needn't handle non-finite values. No bound on the sum of `collapsed` on one device may be relied on, other than what follows from the above.
Results may differ from the reference program's by a relative error of at most 0.0085.
Values may be sent and summed in bfloat16 or wider, within the bound.
A program may use at most 128 MiB of HBM per device.

```python
import math
import jax
import jax.numpy as jnp
import numpy as np
from jax import lax

D = 2048
FF = 768
TOPK = 8
MICRO = 2
TOKM = 24
EXPERTS = 16
TOKENS = 768
CAP = 16
N_REP = 2


def plant(drawn, key, least, largest):
    dims = drawn.shape
    place = [jax.random.randint(jax.random.fold_in(key, axis), (), 0, dims[axis]) for axis in range(len(dims))]
    drawn = drawn.at[tuple(place)].set(least)
    longest = dims.index(max(dims))
    place[longest] = (place[longest] + 1) % dims[longest]
    return drawn.at[tuple(place)].set(largest)


def steps_of(own_key, dims, shards, least, high):
    loudness = 1.0
    for axis_at, shards_of in shards:
        heights = jax.random.uniform(jax.random.fold_in(jax.random.fold_in(own_key, 6), axis_at), (shards_of,), jnp.float32, least / len(shards), high / len(shards))
        loudness = loudness * jnp.repeat(jnp.exp(heights), dims[axis_at] // shards_of).reshape((-1,) + (1,) * (len(dims) - 1 - axis_at))
    return loudness


def routed_block(own_key, own, number, rows, amount, top, limit, lean):
    sequence = jax.random.permutation(own_key, amount)
    packed, common = load_shares(amount, rows * top, limit, lean, True), load_shares(amount, rows * top, limit, lean, False)
    places = jnp.arange(amount)

    def named(lengths, turn):
        used = int((lengths > 0).sum())
        fixed = max(1, used // 4)
        passed = fixed + (places - fixed + turn * (used - fixed)) % max(1, amount - fixed)
        return jnp.zeros((amount,), jnp.int32).at[sequence[jnp.where(places < fixed, places, passed)]].set(jnp.asarray(lengths, jnp.int32))

    lengths = jnp.where(number % 4 == 0, named(packed, number // 4), named(common, number - number // 4 - 1))
    mixed = jax.random.permutation(jax.random.fold_in(own, 3), amount)
    giver, taker = mixed[0:amount // 2 * 2:2], mixed[1:amount // 2 * 2:2]
    slack = jnp.minimum(lengths[giver] - 1, limit - lengths[taker]) // 2
    slack = jnp.where((giver == sequence[0]) | (taker == sequence[0]) | (lengths[taker] == 0), 0, jnp.maximum(slack, 0))
    passed = jax.random.randint(jax.random.fold_in(own, 4), (amount // 2,), 0, 1 << 20) % (slack + 1)
    lengths = lengths.at[giver].add(-passed).at[taker].add(passed)
    items = jnp.searchsorted(jnp.cumsum(lengths), jnp.arange(rows * top), side="right").astype(jnp.int32)
    listing = items.reshape(top, rows).T
    listing = listing[jax.random.permutation(jax.random.fold_in(own, 1), rows)]
    turn = jax.random.randint(jax.random.fold_in(own, 2), (rows, 1), 0, top)
    return jnp.take_along_axis(listing, (jnp.arange(top)[None, :] + turn) % top, axis=1)


def load_shares(number_of, total, most, skew, full):
    weights = [(1 << 20) // math.isqrt(rank ** skew) + 1 for rank in range(1, number_of + 1)]
    largest = most if full else min(most, max(-(-total // number_of), total * weights[0] // sum(weights)))
    least = 1 if total - largest >= number_of - 1 else 0
    given, rest = [largest] + [least] * (number_of - 1), total - largest - least * (number_of - 1)
    while rest > 0:
        free = [i for i in range(1, number_of) if given[i] < largest] or [i for i in range(1, number_of) if given[i] < most]
        pool, left = sum([weights[i] for i in free]), rest
        for i in free:
            addition = min(most - given[i], max(1, left * weights[i] // pool), rest)
            given[i] = given[i] + addition
            rest = rest - addition
    return np.array(given)


def normal_values(rng, dims, spread, most, pieces=(), held_as=jnp.bfloat16):
    level = steps_of(rng, dims, pieces, -0.22, 0.18) if pieces else 1.0
    drawn = jax.random.normal(rng, dims, jnp.float32) * spread * level
    return jnp.minimum(jnp.maximum(drawn, -most), most).astype(held_as)


def setup_inputs(seed: int = 0) -> dict:
    key_of = jax.random.split(jax.random.key(seed), 14)
    tokens = normal_values(key_of[0], (MICRO, TOKENS, D), 1.0, 6.0, ((1, 32),))
    cotangent = normal_values(key_of[1], (MICRO, TOKENS, D), 2.0, 12.0, ((1, 32),))
    routes_keys = jax.random.split(jax.random.fold_in(key_of[2], 1), MICRO * TOKENS // TOKM)
    routes_turns = jax.random.permutation(jax.random.fold_in(key_of[2], 3), MICRO * TOKENS // TOKM)
    routes = jax.vmap(lambda own, number: routed_block(jax.random.fold_in(key_of[2], 2), own, number, TOKM, EXPERTS, TOPK, CAP, 2))(routes_keys, routes_turns).reshape((MICRO, TOKENS, TOPK))
    gates = jnp.clip(0.049804688 + 0.2998047 * jax.random.uniform(key_of[3], (MICRO, TOKENS, TOPK), jnp.float32) ** steps_of(key_of[3], (MICRO, TOKENS, TOPK), ((1, 32),), -0.2, 0.2), 0.049804688, 0.34960938).astype(jnp.bfloat16)
    collapsed = plant((jax.random.randint(key_of[4], (EXPERTS,), 0, 4) < 1).astype(jnp.int32), jax.random.fold_in(key_of[4], 1), 0, 1)
    w_in = normal_values(key_of[5], (EXPERTS, D, 2 * FF), 1.0, 5.0, ((0, 16), (1, 2)))
    w_out = normal_values(key_of[6], (EXPERTS, FF, D), 1.0, 5.0, ((0, 16), (1, 2)))
    first_in = normal_values(key_of[7], (EXPERTS, D, 2 * FF), 0.3, 2.0, ((0, 16), (1, 2)))
    second_in = jnp.clip(jnp.exp(math.log(1.0) - 4.61031033 * jax.random.uniform(key_of[8], (EXPERTS, D, 2 * FF), jnp.float32) ** steps_of(key_of[8], (EXPERTS, D, 2 * FF), ((0, 16), (1, 2)), -0.2, 0.2)), 0.0099487305, 1.0).astype(jnp.bfloat16)
    first_out = normal_values(key_of[9], (EXPERTS, FF, D), 0.3, 2.0, ((0, 16), (1, 2)))
    second_out = jnp.clip(jnp.exp(math.log(1.0) - 4.61031033 * jax.random.uniform(key_of[10], (EXPERTS, FF, D), jnp.float32) ** steps_of(key_of[10], (EXPERTS, FF, D), ((0, 16), (1, 2)), -0.2, 0.2)), 0.0099487305, 1.0).astype(jnp.bfloat16)
    fresh_in = normal_values(key_of[11], (EXPERTS, D, 2 * FF), 1.0, 5.0, ((0, 16), (1, 2)))
    fresh_out = normal_values(key_of[12], (EXPERTS, FF, D), 1.0, 5.0, ((0, 16), (1, 2)))
    return dict(tokens=tokens, cotangent=cotangent, routes=routes, gates=gates, collapsed=collapsed, w_in=w_in, w_out=w_out, first_in=first_in, second_in=second_in, first_out=first_out, second_out=second_out, fresh_in=fresh_in, fresh_out=fresh_out)


beta_one = 0.9
beta_two = 0.95
learn_rate = 0.01
adam_eps = 1e-08
adam_count = 10.0

def silu_parts(gate_half):
    sigmoid_val = jax.nn.sigmoid(gate_half)
    return (gate_half * sigmoid_val, sigmoid_val * (1.0 + gate_half * (1.0 - sigmoid_val)))

def expert_front(rows_in, rows_cot, rows_gate, weight_in, weight_out, scale_in, scale_out):
    hidden = weight_out.shape[0]
    pre_act = jnp.dot(rows_in, weight_in, preferred_element_type=jnp.float32) * scale_in
    gate_half = pre_act[:, :hidden]
    up_half = pre_act[:, hidden:]
    silu_val, slope_val = silu_parts(gate_half)
    active = (silu_val * up_half).astype(jnp.bfloat16)
    result = jnp.dot(active, weight_out, preferred_element_type=jnp.float32) * scale_out
    gate_grad = lax.optimization_barrier(jnp.sum(rows_cot.astype(jnp.float32) * result, axis=1))
    out_cot = (rows_gate.astype(jnp.float32)[:, None] * rows_cot.astype(jnp.float32)).astype(jnp.bfloat16)
    act_cot = lax.dot_general(out_cot, weight_out, (((1,), (1,)), ((), ())), preferred_element_type=jnp.float32) * scale_out
    return (up_half, silu_val, slope_val, act_cot, gate_grad, active, out_cot)

def expert_back(up_half, silu_val, slope_val, act_cot, weight_in, scale_in):
    pre_cot = jnp.concatenate([act_cot * up_half * slope_val, act_cot * silu_val], axis=1).astype(jnp.bfloat16)
    rows_dx = (lax.dot_general(pre_cot, weight_in, (((1,), (1,)), ((), ())), preferred_element_type=jnp.float32) * scale_in).astype(jnp.bfloat16)
    return (pre_cot, rows_dx)

def adam_update(weight, first, second, grad, fresh, dead_flag):
    first_new = beta_one * first.astype(jnp.float32) + (1.0 - beta_one) * grad
    second_new = beta_two * second.astype(jnp.float32) + (1.0 - beta_two) * grad * grad
    first_hat = first_new / (1.0 - beta_one ** adam_count)
    second_hat = second_new / (1.0 - beta_two ** adam_count)
    stepped = weight.astype(jnp.float32) - learn_rate * first_hat / (jnp.sqrt(second_hat) + adam_eps)
    alive_mask = dead_flag == 0
    return (jnp.where(alive_mask, stepped, fresh.astype(jnp.float32)).astype(jnp.bfloat16), jnp.where(alive_mask, first_new, jnp.zeros_like(first_new)).astype(jnp.bfloat16), jnp.where(alive_mask, second_new, jnp.zeros_like(second_new)).astype(jnp.bfloat16))

def slot_ranks(routes):
    blocked = routes.reshape(MICRO, TOKENS // TOKM, TOKM * TOPK)
    onehot = (blocked[..., None] == jnp.arange(EXPERTS, dtype=jnp.int32)).astype(jnp.int32)
    slot_rank = lax.optimization_barrier(jnp.sum((jnp.cumsum(onehot, axis=2) - onehot) * onehot, axis=3))
    return slot_rank.reshape(MICRO, TOKENS, TOPK).astype(jnp.int32)

def reference(tokens, cotangent, routes, gates, collapsed, w_in, w_out, first_in, second_in, first_out, second_out, fresh_in, fresh_out):
    blocks = TOKENS // TOKM
    scale_in = 1.0 / math.sqrt(D)
    scale_out = 1.0 / math.sqrt(FF)
    slot_rank = slot_ranks(routes)
    micro_idx = jnp.broadcast_to(jnp.arange(MICRO, dtype=jnp.int32)[:, None, None], routes.shape)
    token_idx = jnp.broadcast_to(jnp.arange(TOKENS, dtype=jnp.int32)[None, :, None], routes.shape)
    block_idx = (token_idx // TOKM).astype(jnp.int32)
    token_table = jnp.full((MICRO, EXPERTS, blocks, CAP), TOKENS, jnp.int32).at[micro_idx, routes, block_idx, slot_rank].set(token_idx)
    gate_table = jnp.zeros((MICRO, EXPERTS, blocks, CAP), jnp.float32).at[micro_idx, routes, block_idx, slot_rank].set(gates.astype(jnp.float32))

    def per_expert(dx_carry, scan_item):
        expert, weight_in, weight_out, mom_in, var_in, mom_out, var_out, new_in, new_out, dead_flag = scan_item
        grads_in = jnp.zeros((N_REP, D, 2 * FF), jnp.float32)
        grads_out = jnp.zeros((N_REP, FF, D), jnp.float32)
        gate_rows = []
        for which_micro in range(MICRO):
            slot_rows = token_table[which_micro, expert].reshape(-1)
            rows_in = jnp.take(tokens[which_micro], slot_rows, axis=0, mode='fill', fill_value=0)
            rows_cot = jnp.take(cotangent[which_micro], slot_rows, axis=0, mode='fill', fill_value=0)
            rows_gate = gate_table[which_micro, expert].reshape(-1)
            up_half, silu_val, slope_val, act_cot, gate_grad, active, out_cot = expert_front(rows_in, rows_cot, rows_gate, weight_in, weight_out, scale_in, scale_out)
            pre_cot, rows_dx = expert_back(up_half, silu_val, slope_val, act_cot, weight_in, scale_in)
            grads_in = grads_in + jnp.einsum('rnd,rnf->rdf', rows_in.reshape(N_REP, -1, D).astype(jnp.float32), pre_cot.reshape(N_REP, -1, 2 * FF).astype(jnp.float32)) * scale_in
            grads_out = grads_out + jnp.einsum('rnf,rnd->rfd', active.reshape(N_REP, -1, FF).astype(jnp.float32), out_cot.reshape(N_REP, -1, D).astype(jnp.float32)) * scale_out
            dx_carry = dx_carry.at[which_micro, slot_rows].add(rows_dx.astype(jnp.float32), mode='drop')
            gate_rows.append(gate_grad)
        rounded_in = lax.optimization_barrier(grads_in.astype(jnp.bfloat16))
        rounded_out = lax.optimization_barrier(grads_out.astype(jnp.bfloat16))
        grad_in = lax.optimization_barrier(jnp.sum(rounded_in.astype(jnp.float32), axis=0))
        grad_out = lax.optimization_barrier(jnp.sum(rounded_out.astype(jnp.float32), axis=0))
        updated_in = adam_update(weight_in, mom_in, var_in, grad_in, new_in, dead_flag)
        updated_out = adam_update(weight_out, mom_out, var_out, grad_out, new_out, dead_flag)
        return (dx_carry, (jnp.stack(gate_rows), updated_in, updated_out))
    dx_start = jnp.zeros((MICRO, TOKENS, D), jnp.float32)
    dx_sum, (gate_grads, updated_in, updated_out) = lax.scan(per_expert, dx_start, (jnp.arange(EXPERTS, dtype=jnp.int32), w_in, w_out, first_in, second_in, first_out, second_out, fresh_in, fresh_out, collapsed))
    gate_grads = gate_grads.reshape(EXPERTS, MICRO, blocks, CAP)
    d_gates = gate_grads[routes, micro_idx, block_idx, slot_rank].astype(jnp.bfloat16)
    d_tokens = dx_sum.astype(jnp.bfloat16)
    return (d_tokens, d_gates, updated_in[0], updated_out[0], updated_in[1], updated_in[2], updated_out[1], updated_out[2])
```

```python
import math

import jax
import jax.numpy as jnp
from jax import lax
from jax.sharding import PartitionSpec as P

beta_one = 0.9
beta_two = 0.95
learn_rate = 0.01
adam_eps = 1e-08
adam_count = 10.0


def silu_parts(gate_half):
    sigmoid_val = jax.nn.sigmoid(gate_half)
    return (gate_half * sigmoid_val, sigmoid_val * (1.0 + gate_half * (1.0 - sigmoid_val)))


def expert_front(rows_in, rows_cot, rows_gate, weight_in, weight_out, scale_in, scale_out):
    hidden = weight_out.shape[0]
    pre_act = jnp.dot(rows_in, weight_in, preferred_element_type=jnp.float32) * scale_in
    gate_half = pre_act[:, :hidden]
    up_half = pre_act[:, hidden:]
    silu_val, slope_val = silu_parts(gate_half)
    active = (silu_val * up_half).astype(jnp.bfloat16)
    result = jnp.dot(active, weight_out, preferred_element_type=jnp.float32) * scale_out
    gate_grad = jnp.sum(rows_cot.astype(jnp.float32) * result, axis=1)
    out_cot = (rows_gate.astype(jnp.float32)[:, None] * rows_cot.astype(jnp.float32)).astype(
        jnp.bfloat16
    )
    act_cot = (
        lax.dot_general(
            out_cot, weight_out, (((1,), (1,)), ((), ())), preferred_element_type=jnp.float32
        )
        * scale_out
    )
    return (up_half, silu_val, slope_val, act_cot, gate_grad, active, out_cot)


def expert_back(up_half, silu_val, slope_val, act_cot, weight_in, scale_in):
    pre_cot = jnp.concatenate([act_cot * up_half * slope_val, act_cot * silu_val], axis=1).astype(
        jnp.bfloat16
    )
    rows_dx = (
        lax.dot_general(
            pre_cot, weight_in, (((1,), (1,)), ((), ())), preferred_element_type=jnp.float32
        )
        * scale_in
    ).astype(jnp.bfloat16)
    return (pre_cot, rows_dx)


def adam_update(weight, first, second, grad, fresh, dead_flag):
    first_new = beta_one * first.astype(jnp.float32) + (1.0 - beta_one) * grad
    second_new = beta_two * second.astype(jnp.float32) + (1.0 - beta_two) * grad * grad
    first_hat = first_new / (1.0 - beta_one**adam_count)
    second_hat = second_new / (1.0 - beta_two**adam_count)
    stepped = weight.astype(jnp.float32) - learn_rate * first_hat / (
        jnp.sqrt(second_hat) + adam_eps
    )
    alive_mask = dead_flag == 0
    return (
        jnp.where(alive_mask, stepped, fresh.astype(jnp.float32)).astype(jnp.bfloat16),
        jnp.where(alive_mask, first_new, jnp.zeros_like(first_new)).astype(jnp.bfloat16),
        jnp.where(alive_mask, second_new, jnp.zeros_like(second_new)).astype(jnp.bfloat16),
    )


def dispatch_match(route_rows, num_exp, capacity):
    flat_routes = route_rows.reshape(-1)
    onehot = (flat_routes[:, None] == jnp.arange(num_exp, dtype=jnp.int32)[None, :]).astype(
        jnp.int32
    )
    slot_rank = jnp.sum((jnp.cumsum(onehot, axis=0) - onehot) * onehot, axis=1)
    target = (flat_routes * capacity + slot_rank).reshape(route_rows.shape)
    return target[None, :, :] == jnp.arange(num_exp * capacity, dtype=jnp.int32)[:, None, None]


def pack_rows(matched, picker, token_rows, cot_rows, gate_rows, num_exp, capacity):
    sent_in = jnp.dot(picker, token_rows, preferred_element_type=jnp.float32).astype(jnp.bfloat16)
    sent_cot = jnp.dot(picker, cot_rows, preferred_element_type=jnp.float32).astype(jnp.bfloat16)
    sent_gate = jnp.sum(
        jnp.where(matched, gate_rows[None, :, :].astype(jnp.float32), 0.0), axis=(1, 2)
    ).astype(jnp.bfloat16)
    return (
        sent_in.reshape(num_exp, capacity, -1),
        sent_cot.reshape(num_exp, capacity, -1),
        sent_gate.reshape(num_exp, capacity),
    )


def body(
    tokens,
    cotangent,
    routes,
    gates,
    collapsed,
    w_in,
    w_out,
    first_in,
    second_in,
    first_out,
    second_out,
    fresh_in,
    fresh_out,
):
    micro_count, tok_rows, model_width = tokens.shape
    route_width = routes.shape[2]
    sources = lax.axis_size("exp")
    num_exp = w_in.shape[0] * sources
    capacity = min(tok_rows, (4 * tok_rows * route_width + 3 * num_exp - 1) // (3 * num_exp))
    full_in, full_out = (
        lax.all_gather(w_in, "rep", axis=1, tiled=True),
        lax.all_gather(w_out, "rep", axis=1, tiled=True),
    )
    weight_in = full_in[0]
    weight_out = full_out[0]
    hidden = weight_out.shape[0]
    scale_in = 1.0 / math.sqrt(model_width)
    scale_out = 1.0 / math.sqrt(hidden)
    matches = [
        dispatch_match(routes[which_micro], num_exp, capacity) for which_micro in range(micro_count)
    ]
    pickers = [jnp.any(matched, axis=2).astype(jnp.bfloat16) for matched in matches]
    packs = [
        pack_rows(
            matches[which_micro],
            pickers[which_micro],
            tokens[which_micro],
            cotangent[which_micro],
            gates[which_micro],
            num_exp,
            capacity,
        )
        for which_micro in range(micro_count)
    ]
    joined = [jnp.concatenate([packed[member] for packed in packs], axis=1) for member in range(3)]
    arrived = (
        lax.all_to_all(joined[0], "exp", split_axis=0, concat_axis=0, tiled=True),
        lax.all_to_all(joined[1], "exp", split_axis=0, concat_axis=0, tiled=True),
        lax.all_to_all(joined[2], "exp", split_axis=0, concat_axis=0, tiled=True),
    )
    rows_in = arrived[0].reshape(-1, model_width)
    rows_cot = arrived[1].reshape(-1, model_width)
    rows_gate = arrived[2].reshape(-1)
    front_vals = expert_front(
        rows_in, rows_cot, rows_gate, weight_in, weight_out, scale_in, scale_out
    )
    grad_out = (
        lax.dot_general(
            front_vals[5],
            front_vals[6],
            (((0,), (0,)), ((), ())),
            preferred_element_type=jnp.float32,
        )
        * scale_out
    )
    fronts = (rows_in, front_vals)
    rows_in, front_vals = fronts
    pre_cot, rows_dx = expert_back(
        front_vals[0], front_vals[1], front_vals[2], front_vals[3], weight_in, scale_in
    )
    grad_in = (
        lax.dot_general(
            rows_in, pre_cot, (((0,), (0,)), ((), ())), preferred_element_type=jnp.float32
        )
        * scale_in
    )
    back_vals = (rows_dx, front_vals[4].astype(jnp.bfloat16))
    summed_in, summed_out = (
        lax.psum_scatter(
            grad_in[None].astype(jnp.bfloat16), "rep", scatter_dimension=1, tiled=True
        ).astype(jnp.float32),
        lax.psum_scatter(
            grad_out[None].astype(jnp.bfloat16), "rep", scatter_dimension=1, tiled=True
        ).astype(jnp.float32),
    )
    rows_dx, gate_grad = back_vals
    returned = (
        lax.all_to_all(
            rows_dx.reshape(sources, -1, model_width),
            "exp",
            split_axis=0,
            concat_axis=0,
            tiled=True,
        ),
        lax.all_to_all(
            gate_grad.reshape(sources, -1), "exp", split_axis=0, concat_axis=0, tiled=True
        ),
    )
    parts_dx = returned[0].reshape(num_exp, micro_count, capacity, model_width)
    parts_gate = returned[1].reshape(num_exp, micro_count, capacity)
    results = [
        (parts_dx[:, which_micro].reshape(-1, model_width), parts_gate[:, which_micro].reshape(-1))
        for which_micro in range(micro_count)
    ]
    token_dx = []
    token_gate = []
    for which_micro in range(micro_count):
        token_dx.append(
            lax.dot_general(
                pickers[which_micro],
                results[which_micro][0],
                (((0,), (0,)), ((), ())),
                preferred_element_type=jnp.float32,
            ).astype(jnp.bfloat16)
        )
        token_gate.append(
            jnp.sum(
                jnp.where(
                    matches[which_micro],
                    results[which_micro][1].astype(jnp.float32)[:, None, None],
                    0.0,
                ),
                axis=0,
            ).astype(jnp.bfloat16)
        )
    dead_flag = collapsed.reshape(-1, 1, 1)
    updated_in = adam_update(w_in, first_in, second_in, summed_in, fresh_in, dead_flag)
    updated_out = adam_update(w_out, first_out, second_out, summed_out, fresh_out, dead_flag)
    return (
        jnp.stack(token_dx),
        jnp.stack(token_gate),
        updated_in[0],
        updated_out[0],
        updated_in[1],
        updated_in[2],
        updated_out[1],
        updated_out[2],
    )


def partial_body(
    tokens,
    cotangent,
    routes,
    gates,
    collapsed,
    w_in,
    w_out,
    first_in,
    second_in,
    first_out,
    second_out,
    fresh_in,
    fresh_out,
):
    micro, rows, width = tokens.shape
    replicas = lax.axis_size("rep")
    sources = lax.axis_size("exp")
    devices = replicas * sources
    num_exp = sources
    hidden = w_in.shape[2] // 2
    part = hidden // replicas
    me_rep = lax.axis_index("rep")
    me_exp = lax.axis_index("exp")
    scale_in = 1.0 / math.sqrt(width)
    scale_out = 1.0 / math.sqrt(hidden)
    both = ("rep", "exp")
    swap = [(0, 1), (1, 0)]
    depth = w_in.shape[1]

    columns = w_in[0].reshape(depth, 2, replicas, part)
    mine = lax.dynamic_index_in_dim(columns, me_rep, 2, keepdims=False).reshape(depth, 2 * part)
    theirs = lax.dynamic_index_in_dim(columns, 1 - me_rep, 2, keepdims=False).reshape(
        depth, 2 * part
    )
    got = lax.ppermute(theirs, "rep", swap)
    low = me_rep == 0
    weight_in = jnp.concatenate([jnp.where(low, mine, got), jnp.where(low, got, mine)], axis=0)
    weight_out = w_out[0]

    chosen = routes[..., None] == jnp.arange(num_exp, dtype=jnp.int32)
    spread = jnp.sum(jnp.where(chosen, gates[..., None], 0).astype(jnp.float32), axis=2)
    all_gates = lax.all_gather(spread.astype(jnp.bfloat16), both, axis=0)
    all_tokens = lax.all_gather(tokens, both, axis=0).reshape(-1, width)
    all_cots = lax.all_gather(cotangent, both, axis=0).reshape(-1, width)
    is_me = jnp.arange(num_exp, dtype=jnp.int32) == me_exp
    gate = jnp.sum(
        jnp.where(is_me, all_gates.reshape(-1, num_exp).astype(jnp.float32), 0.0),
        axis=1,
        keepdims=True,
    )

    pre = jnp.dot(all_tokens, weight_in, preferred_element_type=jnp.float32) * scale_in
    half, up = pre[:, :part], pre[:, part:]
    silu_val, slope = silu_parts(half)
    active = (silu_val * up).astype(jnp.bfloat16)
    back = (
        lax.dot_general(
            all_cots, weight_out, (((1,), (1,)), ((), ())), preferred_element_type=jnp.float32
        )
        * scale_out
    )
    gate_grad = jnp.sum(active.astype(jnp.float32) * back, axis=1)
    act_cot = back * gate
    pre_cot = jnp.concatenate([act_cot * up * slope, act_cot * silu_val], axis=1).astype(
        jnp.bfloat16
    )
    gated = (active.astype(jnp.float32) * gate).astype(jnp.bfloat16)
    grad_in = (
        lax.dot_general(
            all_tokens, pre_cot, (((0,), (0,)), ((), ())), preferred_element_type=jnp.float32
        )
        * scale_in
    ).astype(jnp.bfloat16)
    sides = grad_in.reshape(replicas, depth, 2 * part)
    own_side = lax.dynamic_index_in_dim(sides, me_rep, 0, keepdims=False)
    far_side = lax.dynamic_index_in_dim(sides, 1 - me_rep, 0, keepdims=False)
    came = lax.ppermute(far_side, "rep", swap)
    rows_dx = (
        lax.dot_general(
            pre_cot, weight_in, (((1,), (1,)), ((), ())), preferred_element_type=jnp.float32
        )
        * scale_in
    ).astype(jnp.bfloat16)
    token_dx = lax.psum_scatter(
        rows_dx.reshape(devices, micro, rows, width), both, scatter_dimension=0, tiled=False
    )
    dense = jnp.where(is_me, gate_grad[:, None], 0.0).reshape(devices, micro * rows * num_exp)
    token_gate = lax.psum_scatter(dense, both, scatter_dimension=0, tiled=False)
    token_gate = token_gate.reshape(micro, rows, 1, num_exp)
    d_gates = jnp.sum(jnp.where(chosen, token_gate, 0.0), axis=3).astype(jnp.bfloat16)
    grad_out = (
        lax.dot_general(
            gated, all_cots, (((0,), (0,)), ((), ())), preferred_element_type=jnp.float32
        )
        * scale_out
    )[None]
    first_cols = jnp.where(low, own_side, came)
    last_cols = jnp.where(low, came, own_side)
    full_grad = jnp.concatenate(
        [first_cols[:, :part], last_cols[:, :part], first_cols[:, part:], last_cols[:, part:]],
        axis=1,
    )[None].astype(jnp.float32)
    dead_flag = collapsed.reshape(-1, 1, 1)
    updated_in = adam_update(w_in, first_in, second_in, full_grad, fresh_in, dead_flag)
    updated_out = adam_update(w_out, first_out, second_out, grad_out, fresh_out, dead_flag)
    return (
        token_dx,
        d_gates,
        updated_in[0],
        updated_out[0],
        updated_in[1],
        updated_in[2],
        updated_out[1],
        updated_out[2],
    )


def solution(mesh):
    inner = partial_body if mesh.shape["rep"] == 2 else body
    placed = (
        P(None, ("rep", "exp"), None),
        P(None, ("rep", "exp"), None),
        P(None, ("rep", "exp"), None),
        P(None, ("rep", "exp"), None),
        P("exp"),
        P("exp", "rep", None),
        P("exp", "rep", None),
        P("exp", "rep", None),
        P("exp", "rep", None),
        P("exp", "rep", None),
        P("exp", "rep", None),
        P("exp", "rep", None),
        P("exp", "rep", None),
    )
    return jax.shard_map(
        inner,
        mesh=mesh,
        in_specs=placed,
        out_specs=(
            P(None, ("rep", "exp"), None),
            P(None, ("rep", "exp"), None),
            P("exp", "rep", None),
            P("exp", "rep", None),
            P("exp", "rep", None),
            P("exp", "rep", None),
            P("exp", "rep", None),
            P("exp", "rep", None),
        ),
        check_vma=False,
    )
```

```python
import math

import jax
import jax.numpy as jnp
from jax import lax
from jax.experimental import pallas as pl
from jax.experimental.pallas import tpu as pltpu
from jax.sharding import PartitionSpec as P

beta_one = 0.9
beta_two = 0.95
learn_rate = 0.01
adam_eps = 1e-08
adam_count = 10.0


def silu_parts(gate_half):
    sigmoid_val = jax.nn.sigmoid(gate_half)
    return (gate_half * sigmoid_val, sigmoid_val * (1.0 + gate_half * (1.0 - sigmoid_val)))


def expert_front(rows_in, rows_cot, rows_gate, weight_in, weight_out, scale_in, scale_out):
    hidden = weight_out.shape[0]
    pre_act = jnp.dot(rows_in, weight_in, preferred_element_type=jnp.float32) * scale_in
    gate_half = pre_act[:, :hidden]
    up_half = pre_act[:, hidden:]
    silu_val, slope_val = silu_parts(gate_half)
    active = (silu_val * up_half).astype(jnp.bfloat16)
    result = jnp.dot(active, weight_out, preferred_element_type=jnp.float32) * scale_out
    gate_grad = jnp.sum(rows_cot.astype(jnp.float32) * result, axis=1)
    out_cot = (rows_gate.astype(jnp.float32)[:, None] * rows_cot.astype(jnp.float32)).astype(
        jnp.bfloat16
    )
    act_cot = (
        lax.dot_general(
            out_cot, weight_out, (((1,), (1,)), ((), ())), preferred_element_type=jnp.float32
        )
        * scale_out
    )
    return (up_half, silu_val, slope_val, act_cot, gate_grad, active, out_cot)


def expert_back(up_half, silu_val, slope_val, act_cot, weight_in, scale_in):
    pre_cot = jnp.concatenate([act_cot * up_half * slope_val, act_cot * silu_val], axis=1).astype(
        jnp.bfloat16
    )
    rows_dx = (
        lax.dot_general(
            pre_cot, weight_in, (((1,), (1,)), ((), ())), preferred_element_type=jnp.float32
        )
        * scale_in
    ).astype(jnp.bfloat16)
    return (pre_cot, rows_dx)


def adam_update(weight, first, second, grad, fresh, dead_flag):
    first_new = beta_one * first.astype(jnp.float32) + (1.0 - beta_one) * grad
    second_new = beta_two * second.astype(jnp.float32) + (1.0 - beta_two) * grad * grad
    first_hat = first_new / (1.0 - beta_one**adam_count)
    second_hat = second_new / (1.0 - beta_two**adam_count)
    stepped = weight.astype(jnp.float32) - learn_rate * first_hat / (
        jnp.sqrt(second_hat) + adam_eps
    )
    alive_mask = dead_flag == 0
    return (
        jnp.where(alive_mask, stepped, fresh.astype(jnp.float32)).astype(jnp.bfloat16),
        jnp.where(alive_mask, first_new, jnp.zeros_like(first_new)).astype(jnp.bfloat16),
        jnp.where(alive_mask, second_new, jnp.zeros_like(second_new)).astype(jnp.bfloat16),
    )


def dispatch_match(route_rows, num_exp, capacity):
    flat_routes = route_rows.reshape(-1)
    onehot = (flat_routes[:, None] == jnp.arange(num_exp, dtype=jnp.int32)[None, :]).astype(
        jnp.int32
    )
    slot_rank = jnp.sum((jnp.cumsum(onehot, axis=0) - onehot) * onehot, axis=1)
    target = (flat_routes * capacity + slot_rank).reshape(route_rows.shape)
    return target[None, :, :] == jnp.arange(num_exp * capacity, dtype=jnp.int32)[:, None, None]


def pack_rows(matched, picker, token_rows, cot_rows, gate_rows, num_exp, capacity):
    sent_in = jnp.dot(picker, token_rows, preferred_element_type=jnp.float32).astype(jnp.bfloat16)
    sent_cot = jnp.dot(picker, cot_rows, preferred_element_type=jnp.float32).astype(jnp.bfloat16)
    sent_gate = jnp.sum(
        jnp.where(matched, gate_rows[None, :, :].astype(jnp.float32), 0.0), axis=(1, 2)
    ).astype(jnp.bfloat16)
    return (
        sent_in.reshape(num_exp, capacity, -1),
        sent_cot.reshape(num_exp, capacity, -1),
        sent_gate.reshape(num_exp, capacity),
    )


def body(
    tokens,
    cotangent,
    routes,
    gates,
    collapsed,
    w_in,
    w_out,
    first_in,
    second_in,
    first_out,
    second_out,
    fresh_in,
    fresh_out,
):
    micro_count, tok_rows, model_width = tokens.shape
    route_width = routes.shape[2]
    sources = lax.axis_size("exp")
    num_exp = w_in.shape[0] * sources
    capacity = min(tok_rows, (4 * tok_rows * route_width + 3 * num_exp - 1) // (3 * num_exp))
    full_in, full_out = (
        lax.all_gather(w_in, "rep", axis=1, tiled=True),
        lax.all_gather(w_out, "rep", axis=1, tiled=True),
    )
    weight_in = full_in[0]
    weight_out = full_out[0]
    hidden = weight_out.shape[0]
    scale_in = 1.0 / math.sqrt(model_width)
    scale_out = 1.0 / math.sqrt(hidden)
    matches = [
        dispatch_match(routes[which_micro], num_exp, capacity) for which_micro in range(micro_count)
    ]
    pickers = [jnp.any(matched, axis=2).astype(jnp.bfloat16) for matched in matches]
    packs = [
        pack_rows(
            matches[which_micro],
            pickers[which_micro],
            tokens[which_micro],
            cotangent[which_micro],
            gates[which_micro],
            num_exp,
            capacity,
        )
        for which_micro in range(micro_count)
    ]
    joined = [jnp.concatenate([packed[member] for packed in packs], axis=1) for member in range(3)]
    arrived = (
        lax.all_to_all(joined[0], "exp", split_axis=0, concat_axis=0, tiled=True),
        lax.all_to_all(joined[1], "exp", split_axis=0, concat_axis=0, tiled=True),
        lax.all_to_all(joined[2], "exp", split_axis=0, concat_axis=0, tiled=True),
    )
    rows_in = arrived[0].reshape(-1, model_width)
    rows_cot = arrived[1].reshape(-1, model_width)
    rows_gate = arrived[2].reshape(-1)
    front_vals = expert_front(
        rows_in, rows_cot, rows_gate, weight_in, weight_out, scale_in, scale_out
    )
    grad_out = (
        lax.dot_general(
            front_vals[5],
            front_vals[6],
            (((0,), (0,)), ((), ())),
            preferred_element_type=jnp.float32,
        )
        * scale_out
    )
    fronts = (rows_in, front_vals)
    rows_in, front_vals = fronts
    pre_cot, rows_dx = expert_back(
        front_vals[0], front_vals[1], front_vals[2], front_vals[3], weight_in, scale_in
    )
    grad_in = (
        lax.dot_general(
            rows_in, pre_cot, (((0,), (0,)), ((), ())), preferred_element_type=jnp.float32
        )
        * scale_in
    )
    back_vals = (rows_dx, front_vals[4].astype(jnp.bfloat16))
    summed_in, summed_out = (
        lax.psum_scatter(
            grad_in[None].astype(jnp.bfloat16), "rep", scatter_dimension=1, tiled=True
        ).astype(jnp.float32),
        lax.psum_scatter(
            grad_out[None].astype(jnp.bfloat16), "rep", scatter_dimension=1, tiled=True
        ).astype(jnp.float32),
    )
    rows_dx, gate_grad = back_vals
    returned = (
        lax.all_to_all(
            rows_dx.reshape(sources, -1, model_width),
            "exp",
            split_axis=0,
            concat_axis=0,
            tiled=True,
        ),
        lax.all_to_all(
            gate_grad.reshape(sources, -1), "exp", split_axis=0, concat_axis=0, tiled=True
        ),
    )
    parts_dx = returned[0].reshape(num_exp, micro_count, capacity, model_width)
    parts_gate = returned[1].reshape(num_exp, micro_count, capacity)
    results = [
        (parts_dx[:, which_micro].reshape(-1, model_width), parts_gate[:, which_micro].reshape(-1))
        for which_micro in range(micro_count)
    ]
    token_dx = []
    token_gate = []
    for which_micro in range(micro_count):
        token_dx.append(
            lax.dot_general(
                pickers[which_micro],
                results[which_micro][0],
                (((0,), (0,)), ((), ())),
                preferred_element_type=jnp.float32,
            ).astype(jnp.bfloat16)
        )
        token_gate.append(
            jnp.sum(
                jnp.where(
                    matches[which_micro],
                    results[which_micro][1].astype(jnp.float32)[:, None, None],
                    0.0,
                ),
                axis=0,
            ).astype(jnp.bfloat16)
        )
    dead_flag = collapsed.reshape(-1, 1, 1)
    updated_in = adam_update(w_in, first_in, second_in, summed_in, fresh_in, dead_flag)
    updated_out = adam_update(w_out, first_out, second_out, summed_out, fresh_out, dead_flag)
    return (
        jnp.stack(token_dx),
        jnp.stack(token_gate),
        updated_in[0],
        updated_out[0],
        updated_in[1],
        updated_in[2],
        updated_out[1],
        updated_out[2],
    )


MESH = pl.DeviceIdType.MESH
Z_SIDE = 4


def where_am_i():
    y = lax.axis_index("rep")
    e = lax.axis_index("exp")
    return y, e // 4, (e // 2) % 2, e % 2


def place_of(here, dy, dz, dx, dc):
    y, z, x, c = here
    return (y + dy) % 2, ((z + dz) % Z_SIDE) * 4 + ((x + dx) % 2) * 2 + (c + dc) % 2


def slot_of(here, dy, dz, dx, dc):
    rep, exp = place_of(here, dy, dz, dx, dc)
    return rep * 16 + exp


def greet(here):
    barrier = pltpu.get_barrier_semaphore()
    near = [(1, 0, 0, 0), (0, 1, 0, 0), (0, 2, 0, 0), (0, 3, 0, 0), (0, 0, 1, 0), (0, 0, 0, 1)]
    for step in near:
        pl.semaphore_signal(barrier, inc=1, device_id=place_of(here, *step), device_id_type=MESH)
    pl.semaphore_wait(barrier, len(near))


def number_of(rel):
    dy, dz, dx, dc = rel
    return dy * 16 + dz * 4 + dx * 2 + dc


def spread_kernel(
    tok_ref, cot_ref, gate_ref, w_ref, tok_all, cot_all, gate_all, w_all, send, recv, local, w_send, w_recv
):
    here = where_am_i()
    y = here[0]
    own = (0, 0, 0, 0)
    ins = (tok_ref, cot_ref, gate_ref)
    outs = (tok_all, cot_all, gate_all)
    depth = w_ref.shape[1]
    part = w_all.shape[1] // 2

    def copy(kind, rel, target, arrives):
        slot = slot_of(here, *rel)
        source = ins[kind] if rel == own else outs[kind].at[slot]
        return pltpu.make_async_remote_copy(
            src_ref=source,
            dst_ref=outs[kind].at[slot],
            send_sem=send.at[kind, number_of(arrives)],
            recv_sem=recv.at[kind, number_of(arrives)],
            device_id=place_of(here, *target),
            device_id_type=MESH,
        )

    sent = []

    def pass_on(rel, kinds=(0, 1, 2)):
        dy, dz, dx, dc = rel
        for kind in kinds:
            goes = []
            if dx == 0:
                goes.append(((0, 0, 1, 0), (dy, dz, 1, 0)))
            if dx == 0 and dy == 0:
                goes.append(((1, 0, 0, 0), (1, dz, 0, 0)))
            if rel == own:
                for step in (1, 3, 2):
                    goes.append(((0, Z_SIDE - step, 0, 0), (0, step, 0, 0)))
            goes.append(((0, 0, 0, 1), (dy, dz, dx, 1)))
            for target, arrives in goes:
                one = copy(kind, rel, target, arrives)
                one.start()
                sent.append(one)

    def landed(kind, rel):
        slot = slot_of(here, *rel)
        pltpu.make_async_remote_copy(
            src_ref=outs[kind].at[slot],
            dst_ref=outs[kind].at[slot],
            send_sem=send.at[kind, number_of(rel)],
            recv_sem=recv.at[kind, number_of(rel)],
            device_id=place_of(here, 0, 0, 0, 1),
            device_id_type=MESH,
        ).wait_recv()

    locals_ = []
    for kind in range(3):
        locals_.append(
            pltpu.make_async_copy(ins[kind], outs[kind].at[slot_of(here, *own)], local.at[kind])
        )
    rows = pl.ds(pl.multiple_of(y * depth, depth), depth)
    for side in range(2):
        locals_.append(
            pltpu.make_async_copy(
                w_ref.at[0, :, pl.ds(pl.multiple_of(side * 2 * part + y * part, 128), part)],
                w_all.at[rows, pl.ds(side * part, part)],
                local.at[3 + side],
            )
        )
    for one in locals_:
        one.start()
    greet(here)
    pass_on(own)
    swaps = []
    for side in range(2):
        swaps.append(
            pltpu.make_async_remote_copy(
                src_ref=w_ref.at[
                    0, :, pl.ds(pl.multiple_of(side * 2 * part + (1 - y) * part, 128), part)
                ],
                dst_ref=w_all.at[rows, pl.ds(side * part, part)],
                send_sem=w_send.at[side],
                recv_sem=w_recv.at[side],
                device_id=place_of(here, 1, 0, 0, 0),
                device_id_type=MESH,
            )
        )
        swaps[-1].start()
    order = [(1, 0, 0, 0), (0, 1, 0, 0), (0, 3, 0, 0), (0, 0, 1, 0), (1, 1, 0, 0), (1, 3, 0, 0)]
    order += [(0, 2, 0, 0), (1, 0, 1, 0), (1, 2, 0, 0)]
    for dz in (1, 3, 2):
        for dy in (0, 1):
            order.append((dy, dz, 1, 0))
    for rel in order:
        for kind in range(3):
            landed(kind, rel)
            pass_on(rel, (kind,))
    for dy in range(2):
        for dz in range(Z_SIDE):
            for dx in range(2):
                for kind in range(3):
                    landed(kind, (dy, dz, dx, 1))
    for one in sent:
        one.wait_send()
    for one in swaps:
        one.wait()
    for one in locals_:
        one.wait()


def spread_all(tok, cot, gate, w_in):
    rows, width = tok.shape
    depth, columns = w_in.shape[1:]
    whole = pl.BlockSpec(memory_space=pl.ANY)
    return pl.pallas_call(
        spread_kernel,
        out_shape=(
            jax.ShapeDtypeStruct((32, rows, width), jnp.bfloat16),
            jax.ShapeDtypeStruct((32, rows, width), jnp.bfloat16),
            jax.ShapeDtypeStruct((32,) + gate.shape, gate.dtype),
            jax.ShapeDtypeStruct((2 * depth, columns // 2), jnp.bfloat16),
        ),
        in_specs=[whole] * 4,
        out_specs=(whole,) * 4,
        scratch_shapes=[
            pltpu.SemaphoreType.DMA((3, 32)),
            pltpu.SemaphoreType.DMA((3, 32)),
            pltpu.SemaphoreType.DMA((5,)),
            pltpu.SemaphoreType.DMA((2,)),
            pltpu.SemaphoreType.DMA((2,)),
        ],
        compiler_params=pltpu.CompilerParams(collective_id=0, has_side_effects=True),
        name="spread_all",
    )(tok, cot, gate, w_in)


def merge_kernel(
    dx_ref,
    dg_ref,
    grad_ref,
    dx_out,
    dg_out,
    grad_out,
    r1x,
    r2x,
    r3x,
    r4x,
    s2x,
    s3x,
    s4x,
    r1g,
    r2g,
    r3g,
    r4g,
    s2g,
    s3g,
    s4g,
    send,
    recv,
    local,
    g_send,
    g_recv,
):
    here = where_am_i()
    y = here[0]
    depth = grad_out.shape[0]
    part = grad_ref.shape[1] // 2
    ins = (dx_ref, dg_ref)
    stage_in = ((r1x, r2x, r3x, r4x), (r1g, r2g, r3g, r4g))
    stage_out = ((None, s2x, s3x, s4x), (None, s2g, s3g, s4g))
    firsts = (0, 16, 24, 28)

    def copy(kind, stage, index, source, target):
        return pltpu.make_async_remote_copy(
            src_ref=source,
            dst_ref=stage_in[kind][stage].at[index],
            send_sem=send.at[kind, firsts[stage] + index],
            recv_sem=recv.at[kind, firsts[stage] + index],
            device_id=place_of(here, *target),
            device_id_type=MESH,
        )

    sent = []

    def go(kind, stage, index, source, target):
        one = copy(kind, stage, index, source, target)
        one.start()
        sent.append(one)

    def landed(kind, stage, index):
        buffer = stage_in[kind][stage].at[index]
        copy(kind, stage, index, buffer, (0, 0, 0, 1)).wait_recv()

    def total(kind, rel, depth_of):
        dy, dz, dx, _ = rel
        value = ins[kind][slot_of(here, *rel)].astype(jnp.float32)
        value = value + stage_in[kind][0][dy * 8 + dz * 2 + dx].astype(jnp.float32)
        if depth_of >= 2:
            value = value + stage_in[kind][1][dy * 4 + dz].astype(jnp.float32)
        if depth_of >= 3:
            value = value + stage_in[kind][2][dz].astype(jnp.float32)
        return value

    columns = [pl.ds(pl.multiple_of(side * 2 * part + y * part, 128), part) for side in range(2)]
    near = pl.ds(pl.multiple_of(y * depth, depth), depth)
    far = pl.ds(pl.multiple_of((1 - y) * depth, depth), depth)
    locals_ = [
        pltpu.make_async_copy(
            grad_ref.at[near, pl.ds(side * part, part)],
            grad_out.at[:, columns[side]],
            local.at[side],
        )
        for side in range(2)
    ]
    for one in locals_:
        one.start()
    greet(here)
    turns = (2, 1, 3, 0)
    for dx in (1, 0):
        for dy in (1, 0):
            for dz in turns:
                for kind in range(2):
                    source = ins[kind].at[slot_of(here, dy, dz, dx, 1)]
                    go(kind, 0, dy * 8 + dz * 2 + dx, source, (0, 0, 0, 1))
    swaps = []
    for side in range(2):
        swaps.append(
            pltpu.make_async_remote_copy(
                src_ref=grad_ref.at[far, pl.ds(side * part, part)],
                dst_ref=grad_out.at[:, columns[side]],
                send_sem=g_send.at[side],
                recv_sem=g_recv.at[side],
                device_id=place_of(here, 1, 0, 0, 0),
                device_id_type=MESH,
            )
        )
        swaps[-1].start()
    for dy in (1, 0):
        for dz in turns:
            for kind in range(2):
                landed(kind, 0, dy * 8 + dz * 2 + 1)
                out = stage_out[kind][1]
                out[dy * 4 + dz] = total(kind, (dy, dz, 1, 0), 1).astype(out.dtype)
                go(kind, 1, dy * 4 + dz, out.at[dy * 4 + dz], (0, 0, 1, 0))
    for dz in turns:
        for kind in range(2):
            landed(kind, 0, 8 + dz * 2)
            landed(kind, 1, 4 + dz)
            out = stage_out[kind][2]
            out[dz] = total(kind, (1, dz, 0, 0), 2).astype(out.dtype)
            go(kind, 2, dz, out.at[dz], (1, 0, 0, 0))
    for dz in turns:
        for kind in range(2):
            landed(kind, 0, dz * 2)
            landed(kind, 1, dz)
            landed(kind, 2, dz)
            if dz:
                out = stage_out[kind][3]
                out[dz - 1] = total(kind, (0, dz, 0, 0), 3).astype(out.dtype)
                go(kind, 3, dz - 1, out.at[dz - 1], (0, dz, 0, 0))
    for kind in range(2):
        value = total(kind, (0, 0, 0, 0), 3)
        for index in range(3):
            landed(kind, 3, index)
            value = value + stage_in[kind][3][index].astype(jnp.float32)
        result = (dx_out, dg_out)[kind]
        result[...] = value.astype(result.dtype)
    for one in sent:
        one.wait_send()
    for one in swaps:
        one.wait()
    for one in locals_:
        one.wait()


def merge_all(dx, dg, grad):
    rows, width = dx.shape[1:]
    depth, columns = grad.shape
    vmem = pl.BlockSpec(memory_space=pltpu.VMEM)
    whole = pl.BlockSpec(memory_space=pl.ANY)
    wide = [pltpu.VMEM((n, rows, width), jnp.bfloat16) for n in (16, 8, 4, 3, 8, 4, 3)]
    small = [pltpu.VMEM((n,) + dg.shape[1:], jnp.float32) for n in (16, 8, 4, 3, 8, 4, 3)]
    return pl.pallas_call(
        merge_kernel,
        out_shape=(
            jax.ShapeDtypeStruct((rows, width), jnp.bfloat16),
            jax.ShapeDtypeStruct(dg.shape[1:], jnp.float32),
            jax.ShapeDtypeStruct((depth // 2, 2 * columns), jnp.bfloat16),
        ),
        in_specs=[vmem, vmem, whole],
        out_specs=(vmem, vmem, whole),
        scratch_shapes=wide
        + small
        + [
            pltpu.SemaphoreType.DMA((2, 31)),
            pltpu.SemaphoreType.DMA((2, 31)),
            pltpu.SemaphoreType.DMA((2,)),
            pltpu.SemaphoreType.DMA((2,)),
            pltpu.SemaphoreType.DMA((2,)),
        ],
        compiler_params=pltpu.CompilerParams(
            collective_id=1, has_side_effects=True, vmem_limit_bytes=40 * 1024 * 1024
        ),
        name="merge_all",
    )(dx, dg, grad)


def partial_body(
    tokens,
    cotangent,
    routes,
    gates,
    collapsed,
    w_in,
    w_out,
    first_in,
    second_in,
    first_out,
    second_out,
    fresh_in,
    fresh_out,
):
    micro, rows, width = tokens.shape
    num_exp = lax.axis_size("exp")
    hidden = w_in.shape[2] // 2
    part = hidden // lax.axis_size("rep")
    me_exp = lax.axis_index("exp")
    scale_in = 1.0 / math.sqrt(width)
    scale_out = 1.0 / math.sqrt(hidden)
    weight_out = w_out[0]
    own_rows = micro * rows
    lanes = 128

    chosen = routes.reshape(own_rows, -1, 1) == jnp.arange(num_exp, dtype=jnp.int32)
    held_gates = gates.reshape(own_rows, -1, 1).astype(jnp.float32)
    spread = jnp.sum(jnp.where(chosen, held_gates, 0.0), axis=1).T
    spread = jnp.pad(spread, ((0, 0), (0, lanes - own_rows))).astype(jnp.bfloat16)
    all_tokens, all_cots, all_gates, weight_in = spread_all(
        tokens.reshape(own_rows, width), cotangent.reshape(own_rows, width), spread, w_in
    )
    all_tokens = all_tokens.reshape(-1, width)
    all_cots = all_cots.reshape(-1, width)
    gate = lax.dynamic_index_in_dim(all_gates, me_exp, 1, keepdims=False)[:, :own_rows]
    gate = gate.astype(jnp.float32).reshape(-1, 1)

    pre = jnp.dot(all_tokens, weight_in, preferred_element_type=jnp.float32) * scale_in
    half, up = pre[:, :part], pre[:, part:]
    silu_val, slope = silu_parts(half)
    active = (silu_val * up).astype(jnp.bfloat16)
    back = (
        lax.dot_general(
            all_cots, weight_out, (((1,), (1,)), ((), ())), preferred_element_type=jnp.float32
        )
        * scale_out
    )
    gate_grad = jnp.sum(active.astype(jnp.float32) * back, axis=1)
    act_cot = back * gate
    pre_cot = jnp.concatenate([act_cot * up * slope, act_cot * silu_val], axis=1).astype(
        jnp.bfloat16
    )
    gated = (active.astype(jnp.float32) * gate).astype(jnp.bfloat16)
    grad_in = (
        lax.dot_general(
            all_tokens, pre_cot, (((0,), (0,)), ((), ())), preferred_element_type=jnp.float32
        )
        * scale_in
    ).astype(jnp.bfloat16)
    rows_dx = (
        lax.dot_general(
            pre_cot, weight_in, (((1,), (1,)), ((), ())), preferred_element_type=jnp.float32
        )
        * scale_in
    ).astype(jnp.bfloat16)
    is_me = jnp.arange(num_exp, dtype=jnp.int32)[:, None] == me_exp
    dense = jnp.pad(gate_grad.reshape(-1, 1, own_rows), ((0, 0), (0, 0), (0, lanes - own_rows)))
    dense = jnp.where(is_me, dense, 0.0)
    token_dx, token_gate, full_grad = merge_all(
        rows_dx.reshape(-1, own_rows, width), dense, grad_in
    )
    token_dx = token_dx.reshape(micro, rows, width)
    token_gate = token_gate[:, :own_rows].T[:, None, :]
    d_gates = jnp.sum(jnp.where(chosen, token_gate, 0.0), axis=2).astype(jnp.bfloat16)
    d_gates = d_gates.reshape(gates.shape)
    grad_out = (
        lax.dot_general(
            gated, all_cots, (((0,), (0,)), ((), ())), preferred_element_type=jnp.float32
        )
        * scale_out
    )[None]
    full_grad = full_grad[None].astype(jnp.float32)
    dead_flag = collapsed.reshape(-1, 1, 1)
    updated_in = adam_update(w_in, first_in, second_in, full_grad, fresh_in, dead_flag)
    updated_out = adam_update(w_out, first_out, second_out, grad_out, fresh_out, dead_flag)
    return (
        token_dx,
        d_gates,
        updated_in[0],
        updated_out[0],
        updated_in[1],
        updated_in[2],
        updated_out[1],
        updated_out[2],
    )


def solution(mesh):
    narrow = mesh.shape["rep"] == 2 and mesh.shape["exp"] == 16
    inner = partial_body if narrow else body
    placed = (
        P(None, ("rep", "exp"), None),
        P(None, ("rep", "exp"), None),
        P(None, ("rep", "exp"), None),
        P(None, ("rep", "exp"), None),
        P("exp"),
        P("exp", "rep", None),
        P("exp", "rep", None),
        P("exp", "rep", None),
        P("exp", "rep", None),
        P("exp", "rep", None),
        P("exp", "rep", None),
        P("exp", "rep", None),
        P("exp", "rep", None),
    )
    return jax.shard_map(
        inner,
        mesh=mesh,
        in_specs=placed,
        out_specs=(
            P(None, ("rep", "exp"), None),
            P(None, ("rep", "exp"), None),
            P("exp", "rep", None),
            P("exp", "rep", None),
            P("exp", "rep", None),
            P("exp", "rep", None),
            P("exp", "rep", None),
            P("exp", "rep", None),
        ),
        check_vma=False,
    )
```

```python
import math

import jax
import jax.numpy as jnp
from jax import lax
from jax.experimental import pallas as pl
from jax.experimental.pallas import tpu as pltpu
from jax.sharding import PartitionSpec as P

beta_one = 0.9
beta_two = 0.95
learn_rate = 0.01
adam_eps = 1e-08
adam_count = 10.0


def silu_parts(gate_half):
    sigmoid_val = jax.nn.sigmoid(gate_half)
    return (gate_half * sigmoid_val, sigmoid_val * (1.0 + gate_half * (1.0 - sigmoid_val)))


def expert_front(rows_in, rows_cot, rows_gate, weight_in, weight_out, scale_in, scale_out):
    hidden = weight_out.shape[0]
    pre_act = jnp.dot(rows_in, weight_in, preferred_element_type=jnp.float32) * scale_in
    gate_half = pre_act[:, :hidden]
    up_half = pre_act[:, hidden:]
    silu_val, slope_val = silu_parts(gate_half)
    active = (silu_val * up_half).astype(jnp.bfloat16)
    result = jnp.dot(active, weight_out, preferred_element_type=jnp.float32) * scale_out
    gate_grad = jnp.sum(rows_cot.astype(jnp.float32) * result, axis=1)
    out_cot = (rows_gate.astype(jnp.float32)[:, None] * rows_cot.astype(jnp.float32)).astype(
        jnp.bfloat16
    )
    act_cot = (
        lax.dot_general(
            out_cot, weight_out, (((1,), (1,)), ((), ())), preferred_element_type=jnp.float32
        )
        * scale_out
    )
    return (up_half, silu_val, slope_val, act_cot, gate_grad, active, out_cot)


def expert_back(up_half, silu_val, slope_val, act_cot, weight_in, scale_in):
    pre_cot = jnp.concatenate([act_cot * up_half * slope_val, act_cot * silu_val], axis=1).astype(
        jnp.bfloat16
    )
    rows_dx = (
        lax.dot_general(
            pre_cot, weight_in, (((1,), (1,)), ((), ())), preferred_element_type=jnp.float32
        )
        * scale_in
    ).astype(jnp.bfloat16)
    return (pre_cot, rows_dx)


def adam_update(weight, first, second, grad, fresh, dead_flag):
    first_new = beta_one * first.astype(jnp.float32) + (1.0 - beta_one) * grad
    second_new = beta_two * second.astype(jnp.float32) + (1.0 - beta_two) * grad * grad
    first_hat = first_new / (1.0 - beta_one**adam_count)
    second_hat = second_new / (1.0 - beta_two**adam_count)
    stepped = weight.astype(jnp.float32) - learn_rate * first_hat / (
        jnp.sqrt(second_hat) + adam_eps
    )
    alive_mask = dead_flag == 0
    return (
        jnp.where(alive_mask, stepped, fresh.astype(jnp.float32)).astype(jnp.bfloat16),
        jnp.where(alive_mask, first_new, jnp.zeros_like(first_new)).astype(jnp.bfloat16),
        jnp.where(alive_mask, second_new, jnp.zeros_like(second_new)).astype(jnp.bfloat16),
    )


def dispatch_match(route_rows, num_exp, capacity):
    flat_routes = route_rows.reshape(-1)
    onehot = (flat_routes[:, None] == jnp.arange(num_exp, dtype=jnp.int32)[None, :]).astype(
        jnp.int32
    )
    slot_rank = jnp.sum((jnp.cumsum(onehot, axis=0) - onehot) * onehot, axis=1)
    target = (flat_routes * capacity + slot_rank).reshape(route_rows.shape)
    return target[None, :, :] == jnp.arange(num_exp * capacity, dtype=jnp.int32)[:, None, None]


def pack_rows(matched, picker, token_rows, cot_rows, gate_rows, num_exp, capacity):
    sent_in = jnp.dot(picker, token_rows, preferred_element_type=jnp.float32).astype(jnp.bfloat16)
    sent_cot = jnp.dot(picker, cot_rows, preferred_element_type=jnp.float32).astype(jnp.bfloat16)
    sent_gate = jnp.sum(
        jnp.where(matched, gate_rows[None, :, :].astype(jnp.float32), 0.0), axis=(1, 2)
    ).astype(jnp.bfloat16)
    return (
        sent_in.reshape(num_exp, capacity, -1),
        sent_cot.reshape(num_exp, capacity, -1),
        sent_gate.reshape(num_exp, capacity),
    )


def body(
    tokens,
    cotangent,
    routes,
    gates,
    collapsed,
    w_in,
    w_out,
    first_in,
    second_in,
    first_out,
    second_out,
    fresh_in,
    fresh_out,
):
    micro_count, tok_rows, model_width = tokens.shape
    route_width = routes.shape[2]
    sources = lax.axis_size("exp")
    num_exp = w_in.shape[0] * sources
    capacity = min(tok_rows, (4 * tok_rows * route_width + 3 * num_exp - 1) // (3 * num_exp))
    full_in, full_out = (
        lax.all_gather(w_in, "rep", axis=1, tiled=True),
        lax.all_gather(w_out, "rep", axis=1, tiled=True),
    )
    weight_in = full_in[0]
    weight_out = full_out[0]
    hidden = weight_out.shape[0]
    scale_in = 1.0 / math.sqrt(model_width)
    scale_out = 1.0 / math.sqrt(hidden)
    matches = [
        dispatch_match(routes[which_micro], num_exp, capacity) for which_micro in range(micro_count)
    ]
    pickers = [jnp.any(matched, axis=2).astype(jnp.bfloat16) for matched in matches]
    packs = [
        pack_rows(
            matches[which_micro],
            pickers[which_micro],
            tokens[which_micro],
            cotangent[which_micro],
            gates[which_micro],
            num_exp,
            capacity,
        )
        for which_micro in range(micro_count)
    ]
    joined = [jnp.concatenate([packed[member] for packed in packs], axis=1) for member in range(3)]
    arrived = (
        lax.all_to_all(joined[0], "exp", split_axis=0, concat_axis=0, tiled=True),
        lax.all_to_all(joined[1], "exp", split_axis=0, concat_axis=0, tiled=True),
        lax.all_to_all(joined[2], "exp", split_axis=0, concat_axis=0, tiled=True),
    )
    rows_in = arrived[0].reshape(-1, model_width)
    rows_cot = arrived[1].reshape(-1, model_width)
    rows_gate = arrived[2].reshape(-1)
    front_vals = expert_front(
        rows_in, rows_cot, rows_gate, weight_in, weight_out, scale_in, scale_out
    )
    grad_out = (
        lax.dot_general(
            front_vals[5],
            front_vals[6],
            (((0,), (0,)), ((), ())),
            preferred_element_type=jnp.float32,
        )
        * scale_out
    )
    fronts = (rows_in, front_vals)
    rows_in, front_vals = fronts
    pre_cot, rows_dx = expert_back(
        front_vals[0], front_vals[1], front_vals[2], front_vals[3], weight_in, scale_in
    )
    grad_in = (
        lax.dot_general(
            rows_in, pre_cot, (((0,), (0,)), ((), ())), preferred_element_type=jnp.float32
        )
        * scale_in
    )
    back_vals = (rows_dx, front_vals[4].astype(jnp.bfloat16))
    summed_in, summed_out = (
        lax.psum_scatter(
            grad_in[None].astype(jnp.bfloat16), "rep", scatter_dimension=1, tiled=True
        ).astype(jnp.float32),
        lax.psum_scatter(
            grad_out[None].astype(jnp.bfloat16), "rep", scatter_dimension=1, tiled=True
        ).astype(jnp.float32),
    )
    rows_dx, gate_grad = back_vals
    returned = (
        lax.all_to_all(
            rows_dx.reshape(sources, -1, model_width),
            "exp",
            split_axis=0,
            concat_axis=0,
            tiled=True,
        ),
        lax.all_to_all(
            gate_grad.reshape(sources, -1), "exp", split_axis=0, concat_axis=0, tiled=True
        ),
    )
    parts_dx = returned[0].reshape(num_exp, micro_count, capacity, model_width)
    parts_gate = returned[1].reshape(num_exp, micro_count, capacity)
    results = [
        (parts_dx[:, which_micro].reshape(-1, model_width), parts_gate[:, which_micro].reshape(-1))
        for which_micro in range(micro_count)
    ]
    token_dx = []
    token_gate = []
    for which_micro in range(micro_count):
        token_dx.append(
            lax.dot_general(
                pickers[which_micro],
                results[which_micro][0],
                (((0,), (0,)), ((), ())),
                preferred_element_type=jnp.float32,
            ).astype(jnp.bfloat16)
        )
        token_gate.append(
            jnp.sum(
                jnp.where(
                    matches[which_micro],
                    results[which_micro][1].astype(jnp.float32)[:, None, None],
                    0.0,
                ),
                axis=0,
            ).astype(jnp.bfloat16)
        )
    dead_flag = collapsed.reshape(-1, 1, 1)
    updated_in = adam_update(w_in, first_in, second_in, summed_in, fresh_in, dead_flag)
    updated_out = adam_update(w_out, first_out, second_out, summed_out, fresh_out, dead_flag)
    return (
        jnp.stack(token_dx),
        jnp.stack(token_gate),
        updated_in[0],
        updated_out[0],
        updated_in[1],
        updated_in[2],
        updated_out[1],
        updated_out[2],
    )


MESH = pl.DeviceIdType.MESH
Z_SIDE = 4


def where_am_i():
    y = lax.axis_index("rep")
    e = lax.axis_index("exp")
    return y, e // 4, (e // 2) % 2, e % 2


def place_of(here, dy, dz, dx, dc):
    y, z, x, c = here
    return (y + dy) % 2, ((z + dz) % Z_SIDE) * 4 + ((x + dx) % 2) * 2 + (c + dc) % 2


def slot_of(here, dy, dz, dx, dc):
    rep, exp = place_of(here, dy, dz, dx, dc)
    return rep * 16 + exp


def greet(here):
    barrier = pltpu.get_barrier_semaphore()
    near = [(1, 0, 0, 0), (0, 1, 0, 0), (0, 2, 0, 0), (0, 3, 0, 0), (0, 0, 1, 0), (0, 0, 0, 1)]
    for step in near:
        pl.semaphore_signal(barrier, inc=1, device_id=place_of(here, *step), device_id_type=MESH)
    pl.semaphore_wait(barrier, len(near))


def number_of(rel):
    dy, dz, dx, dc = rel
    return dy * 16 + dz * 4 + dx * 2 + dc


def spread_kernel(
    tok_ref, cot_ref, gate_ref, w_ref, tok_all, cot_all, gate_all, w_all, send, recv, local, w_send, w_recv
):
    here = where_am_i()
    y = here[0]
    own = (0, 0, 0, 0)
    ins = (tok_ref, cot_ref, gate_ref)
    outs = (tok_all, cot_all, gate_all)
    depth = w_ref.shape[1]
    part = w_all.shape[1] // 2

    def copy(kind, rel, target, arrives):
        slot = slot_of(here, *rel)
        source = ins[kind] if rel == own else outs[kind].at[slot]
        return pltpu.make_async_remote_copy(
            src_ref=source,
            dst_ref=outs[kind].at[slot],
            send_sem=send.at[kind, number_of(arrives)],
            recv_sem=recv.at[kind, number_of(arrives)],
            device_id=place_of(here, *target),
            device_id_type=MESH,
        )

    sent = []

    def pass_on(rel, kinds=(0, 1, 2)):
        dy, dz, dx, dc = rel
        for kind in kinds:
            goes = []
            if dx == 0:
                goes.append(((0, 0, 1, 0), (dy, dz, 1, 0)))
            if dx == 0 and dy == 0 and (kind != 1 or dz == 0):
                goes.append(((1, 0, 0, 0), (1, dz, 0, 0)))
            if rel == own or (kind == 1 and dx == 0 and dz == 0):
                for step in (1, 3, 2):
                    goes.append(((0, Z_SIDE - step, 0, 0), (dy, step, 0, 0)))
            goes.append(((0, 0, 0, 1), (dy, dz, dx, 1)))
            for target, arrives in goes:
                one = copy(kind, rel, target, arrives)
                one.start()
                sent.append(one)

    def landed(kind, rel):
        slot = slot_of(here, *rel)
        pltpu.make_async_remote_copy(
            src_ref=outs[kind].at[slot],
            dst_ref=outs[kind].at[slot],
            send_sem=send.at[kind, number_of(rel)],
            recv_sem=recv.at[kind, number_of(rel)],
            device_id=place_of(here, 0, 0, 0, 1),
            device_id_type=MESH,
        ).wait_recv()

    locals_ = []
    for kind in range(3):
        locals_.append(
            pltpu.make_async_copy(ins[kind], outs[kind].at[slot_of(here, *own)], local.at[kind])
        )
    rows = pl.ds(pl.multiple_of(y * depth, depth), depth)
    for side in range(2):
        locals_.append(
            pltpu.make_async_copy(
                w_ref.at[0, :, pl.ds(pl.multiple_of(side * 2 * part + y * part, 128), part)],
                w_all.at[rows, pl.ds(side * part, part)],
                local.at[3 + side],
            )
        )
    for one in locals_:
        one.start()
    greet(here)
    pass_on(own)
    swaps = []
    for side in range(2):
        swaps.append(
            pltpu.make_async_remote_copy(
                src_ref=w_ref.at[
                    0, :, pl.ds(pl.multiple_of(side * 2 * part + (1 - y) * part, 128), part)
                ],
                dst_ref=w_all.at[rows, pl.ds(side * part, part)],
                send_sem=w_send.at[side],
                recv_sem=w_recv.at[side],
                device_id=place_of(here, 1, 0, 0, 0),
                device_id_type=MESH,
            )
        )
        swaps[-1].start()
    order = [(1, 0, 0, 0), (0, 1, 0, 0), (0, 3, 0, 0), (0, 0, 1, 0), (1, 1, 0, 0), (1, 3, 0, 0)]
    order += [(0, 2, 0, 0), (1, 0, 1, 0), (1, 2, 0, 0)]
    for dz in (1, 3, 2):
        for dy in (0, 1):
            order.append((dy, dz, 1, 0))
    for rel in order:
        for kind in range(3):
            landed(kind, rel)
            pass_on(rel, (kind,))
    for dy in range(2):
        for dz in range(Z_SIDE):
            for dx in range(2):
                for kind in range(3):
                    landed(kind, (dy, dz, dx, 1))
    for one in sent:
        one.wait_send()
    for one in swaps:
        one.wait()
    for one in locals_:
        one.wait()


def spread_all(tok, cot, gate, w_in):
    rows, width = tok.shape
    depth, columns = w_in.shape[1:]
    whole = pl.BlockSpec(memory_space=pl.ANY)
    return pl.pallas_call(
        spread_kernel,
        out_shape=(
            jax.ShapeDtypeStruct((32, rows, width), jnp.bfloat16),
            jax.ShapeDtypeStruct((32, rows, width), jnp.bfloat16),
            jax.ShapeDtypeStruct((32,) + gate.shape, gate.dtype),
            jax.ShapeDtypeStruct((2 * depth, columns // 2), jnp.bfloat16),
        ),
        in_specs=[whole] * 4,
        out_specs=(whole,) * 4,
        scratch_shapes=[
            pltpu.SemaphoreType.DMA((3, 32)),
            pltpu.SemaphoreType.DMA((3, 32)),
            pltpu.SemaphoreType.DMA((5,)),
            pltpu.SemaphoreType.DMA((2,)),
            pltpu.SemaphoreType.DMA((2,)),
        ],
        compiler_params=pltpu.CompilerParams(collective_id=0, has_side_effects=True),
        name="spread_all",
    )(tok, cot, gate, w_in)


def merge_kernel(
    dx_ref,
    dg_ref,
    grad_ref,
    dx_out,
    dg_out,
    grad_out,
    r1x,
    r2x,
    r3x,
    r4x,
    s2x,
    s3x,
    s4x,
    r1g,
    r2g,
    r3g,
    r4g,
    s2g,
    s3g,
    s4g,
    send,
    recv,
    local,
    g_send,
    g_recv,
):
    here = where_am_i()
    y = here[0]
    depth = grad_out.shape[0]
    part = grad_ref.shape[1] // 2
    ins = (dx_ref, dg_ref)
    stage_in = ((r1x, r2x, r3x, r4x), (r1g, r2g, r3g, r4g))
    stage_out = ((None, s2x, s3x, s4x), (None, s2g, s3g, s4g))
    firsts = (0, 16, 24, 30)

    def copy(kind, stage, index, source, target):
        return pltpu.make_async_remote_copy(
            src_ref=source,
            dst_ref=stage_in[kind][stage].at[index],
            send_sem=send.at[kind, firsts[stage] + index],
            recv_sem=recv.at[kind, firsts[stage] + index],
            device_id=place_of(here, *target),
            device_id_type=MESH,
        )

    sent = []

    def go(kind, stage, index, source, target):
        one = copy(kind, stage, index, source, target)
        one.start()
        sent.append(one)

    def landed(kind, stage, index):
        buffer = stage_in[kind][stage].at[index]
        copy(kind, stage, index, buffer, (0, 0, 0, 1)).wait_recv()

    def total(kind, rel, depth_of):
        dy, dz, dx, _ = rel
        value = ins[kind][slot_of(here, *rel)].astype(jnp.float32)
        value = value + stage_in[kind][0][dy * 8 + dz * 2 + dx].astype(jnp.float32)
        if depth_of >= 2:
            value = value + stage_in[kind][1][dy * 4 + dz].astype(jnp.float32)
        if depth_of >= 3:
            for index in range(3):
                value = value + stage_in[kind][2][dy * 3 + index].astype(jnp.float32)
        return value

    columns = [pl.ds(pl.multiple_of(side * 2 * part + y * part, 128), part) for side in range(2)]
    near = pl.ds(pl.multiple_of(y * depth, depth), depth)
    far = pl.ds(pl.multiple_of((1 - y) * depth, depth), depth)
    locals_ = [
        pltpu.make_async_copy(
            grad_ref.at[near, pl.ds(side * part, part)],
            grad_out.at[:, columns[side]],
            local.at[side],
        )
        for side in range(2)
    ]
    for one in locals_:
        one.start()
    greet(here)
    turns = ((1, 2), (1, 1), (1, 3), (0, 2), (0, 1), (0, 3), (1, 0), (0, 0))
    for dx in (1, 0):
        for dy, dz in turns:
            for kind in range(2):
                source = ins[kind].at[slot_of(here, dy, dz, dx, 1)]
                go(kind, 0, dy * 8 + dz * 2 + dx, source, (0, 0, 0, 1))
    swaps = []
    for side in range(2):
        swaps.append(
            pltpu.make_async_remote_copy(
                src_ref=grad_ref.at[far, pl.ds(side * part, part)],
                dst_ref=grad_out.at[:, columns[side]],
                send_sem=g_send.at[side],
                recv_sem=g_recv.at[side],
                device_id=place_of(here, 1, 0, 0, 0),
                device_id_type=MESH,
            )
        )
        swaps[-1].start()
    for dy, dz in turns:
        for kind in range(2):
            landed(kind, 0, dy * 8 + dz * 2 + 1)
            out = stage_out[kind][1]
            out[dy * 4 + dz] = total(kind, (dy, dz, 1, 0), 1).astype(out.dtype)
            go(kind, 1, dy * 4 + dz, out.at[dy * 4 + dz], (0, 0, 1, 0))
    for dy, dz in turns:
        for kind in range(2):
            landed(kind, 0, dy * 8 + dz * 2)
            landed(kind, 1, dy * 4 + dz)
            if dz:
                index = dy * 3 + dz - 1
                out = stage_out[kind][2]
                out[index] = total(kind, (dy, dz, 0, 0), 2).astype(out.dtype)
                go(kind, 2, index, out.at[index], (0, dz, 0, 0))
    for kind in range(2):
        for index in range(3):
            landed(kind, 2, 3 + index)
        out = stage_out[kind][3]
        out[0] = total(kind, (1, 0, 0, 0), 3).astype(out.dtype)
        go(kind, 3, 0, out.at[0], (1, 0, 0, 0))
    for kind in range(2):
        for index in range(3):
            landed(kind, 2, index)
        value = total(kind, (0, 0, 0, 0), 3)
        landed(kind, 3, 0)
        value = value + stage_in[kind][3][0].astype(jnp.float32)
        result = (dx_out, dg_out)[kind]
        result[...] = value.astype(result.dtype)
    for one in sent:
        one.wait_send()
    for one in swaps:
        one.wait()
    for one in locals_:
        one.wait()


def merge_all(dx, dg, grad):
    rows, width = dx.shape[1:]
    depth, columns = grad.shape
    vmem = pl.BlockSpec(memory_space=pltpu.VMEM)
    whole = pl.BlockSpec(memory_space=pl.ANY)
    wide = [pltpu.VMEM((n, rows, width), jnp.bfloat16) for n in (16, 8, 6, 1, 8, 6, 1)]
    small = [pltpu.VMEM((n,) + dg.shape[1:], jnp.float32) for n in (16, 8, 6, 1, 8, 6, 1)]
    return pl.pallas_call(
        merge_kernel,
        out_shape=(
            jax.ShapeDtypeStruct((rows, width), jnp.bfloat16),
            jax.ShapeDtypeStruct(dg.shape[1:], jnp.float32),
            jax.ShapeDtypeStruct((depth // 2, 2 * columns), jnp.bfloat16),
        ),
        in_specs=[vmem, vmem, whole],
        out_specs=(vmem, vmem, whole),
        scratch_shapes=wide
        + small
        + [
            pltpu.SemaphoreType.DMA((2, 31)),
            pltpu.SemaphoreType.DMA((2, 31)),
            pltpu.SemaphoreType.DMA((2,)),
            pltpu.SemaphoreType.DMA((2,)),
            pltpu.SemaphoreType.DMA((2,)),
        ],
        compiler_params=pltpu.CompilerParams(
            collective_id=1, has_side_effects=True, vmem_limit_bytes=40 * 1024 * 1024
        ),
        name="merge_all",
    )(dx, dg, grad)


def partial_body(
    tokens,
    cotangent,
    routes,
    gates,
    collapsed,
    w_in,
    w_out,
    first_in,
    second_in,
    first_out,
    second_out,
    fresh_in,
    fresh_out,
):
    micro, rows, width = tokens.shape
    num_exp = lax.axis_size("exp")
    hidden = w_in.shape[2] // 2
    part = hidden // lax.axis_size("rep")
    me_exp = lax.axis_index("exp")
    scale_in = 1.0 / math.sqrt(width)
    scale_out = 1.0 / math.sqrt(hidden)
    weight_out = w_out[0]
    own_rows = micro * rows
    lanes = 128

    chosen = routes.reshape(own_rows, -1, 1) == jnp.arange(num_exp, dtype=jnp.int32)
    held_gates = gates.reshape(own_rows, -1, 1).astype(jnp.float32)
    spread = jnp.sum(jnp.where(chosen, held_gates, 0.0), axis=1).T
    spread = jnp.pad(spread, ((0, 0), (0, lanes - own_rows))).astype(jnp.bfloat16)
    all_tokens, all_cots, all_gates, weight_in = spread_all(
        tokens.reshape(own_rows, width), cotangent.reshape(own_rows, width), spread, w_in
    )
    all_tokens = all_tokens.reshape(-1, width)
    all_cots = all_cots.reshape(-1, width)
    gate = lax.dynamic_index_in_dim(all_gates, me_exp, 1, keepdims=False)[:, :own_rows]
    gate = gate.astype(jnp.float32).reshape(-1, 1)

    pre = jnp.dot(all_tokens, weight_in, preferred_element_type=jnp.float32) * scale_in
    half, up = pre[:, :part], pre[:, part:]
    silu_val, slope = silu_parts(half)
    active = (silu_val * up).astype(jnp.bfloat16)
    back = (
        lax.dot_general(
            all_cots, weight_out, (((1,), (1,)), ((), ())), preferred_element_type=jnp.float32
        )
        * scale_out
    )
    gate_grad = jnp.sum(active.astype(jnp.float32) * back, axis=1)
    act_cot = back * gate
    pre_cot = jnp.concatenate([act_cot * up * slope, act_cot * silu_val], axis=1).astype(
        jnp.bfloat16
    )
    gated = (active.astype(jnp.float32) * gate).astype(jnp.bfloat16)
    grad_in = (
        lax.dot_general(
            all_tokens, pre_cot, (((0,), (0,)), ((), ())), preferred_element_type=jnp.float32
        )
        * scale_in
    ).astype(jnp.bfloat16)
    rows_dx = (
        lax.dot_general(
            pre_cot, weight_in, (((1,), (1,)), ((), ())), preferred_element_type=jnp.float32
        )
        * scale_in
    ).astype(jnp.bfloat16)
    is_me = jnp.arange(num_exp, dtype=jnp.int32)[:, None] == me_exp
    dense = jnp.pad(gate_grad.reshape(-1, 1, own_rows), ((0, 0), (0, 0), (0, lanes - own_rows)))
    dense = jnp.where(is_me, dense, 0.0)
    token_dx, token_gate, full_grad = merge_all(
        rows_dx.reshape(-1, own_rows, width), dense, grad_in
    )
    token_dx = token_dx.reshape(micro, rows, width)
    token_gate = token_gate[:, :own_rows].T[:, None, :]
    d_gates = jnp.sum(jnp.where(chosen, token_gate, 0.0), axis=2).astype(jnp.bfloat16)
    d_gates = d_gates.reshape(gates.shape)
    grad_out = (
        lax.dot_general(
            gated, all_cots, (((0,), (0,)), ((), ())), preferred_element_type=jnp.float32
        )
        * scale_out
    )[None]
    full_grad = full_grad[None].astype(jnp.float32)
    dead_flag = collapsed.reshape(-1, 1, 1)
    updated_in = adam_update(w_in, first_in, second_in, full_grad, fresh_in, dead_flag)
    updated_out = adam_update(w_out, first_out, second_out, grad_out, fresh_out, dead_flag)
    return (
        token_dx,
        d_gates,
        updated_in[0],
        updated_out[0],
        updated_in[1],
        updated_in[2],
        updated_out[1],
        updated_out[2],
    )


def solution(mesh):
    narrow = mesh.shape["rep"] == 2 and mesh.shape["exp"] == 16
    inner = partial_body if narrow else body
    placed = (
        P(None, ("rep", "exp"), None),
        P(None, ("rep", "exp"), None),
        P(None, ("rep", "exp"), None),
        P(None, ("rep", "exp"), None),
        P("exp"),
        P("exp", "rep", None),
        P("exp", "rep", None),
        P("exp", "rep", None),
        P("exp", "rep", None),
        P("exp", "rep", None),
        P("exp", "rep", None),
        P("exp", "rep", None),
        P("exp", "rep", None),
    )
    return jax.shard_map(
        inner,
        mesh=mesh,
        in_specs=placed,
        out_specs=(
            P(None, ("rep", "exp"), None),
            P(None, ("rep", "exp"), None),
            P("exp", "rep", None),
            P("exp", "rep", None),
            P("exp", "rep", None),
            P("exp", "rep", None),
            P("exp", "rep", None),
            P("exp", "rep", None),
        ),
        check_vma=False,
    )
```

```python
import math

import jax
import jax.numpy as jnp
from jax import lax
from jax.experimental import pallas as pl
from jax.experimental.pallas import tpu as pltpu
from jax.sharding import PartitionSpec as P

beta_one = 0.9
beta_two = 0.95
learn_rate = 0.01
adam_eps = 1e-08
adam_count = 10.0


def silu_parts(gate_half):
    sigmoid_val = jax.nn.sigmoid(gate_half)
    return (gate_half * sigmoid_val, sigmoid_val * (1.0 + gate_half * (1.0 - sigmoid_val)))


def expert_front(rows_in, rows_cot, rows_gate, weight_in, weight_out, scale_in, scale_out):
    hidden = weight_out.shape[0]
    pre_act = jnp.dot(rows_in, weight_in, preferred_element_type=jnp.float32) * scale_in
    gate_half = pre_act[:, :hidden]
    up_half = pre_act[:, hidden:]
    silu_val, slope_val = silu_parts(gate_half)
    active = (silu_val * up_half).astype(jnp.bfloat16)
    result = jnp.dot(active, weight_out, preferred_element_type=jnp.float32) * scale_out
    gate_grad = jnp.sum(rows_cot.astype(jnp.float32) * result, axis=1)
    out_cot = (rows_gate.astype(jnp.float32)[:, None] * rows_cot.astype(jnp.float32)).astype(
        jnp.bfloat16
    )
    act_cot = (
        lax.dot_general(
            out_cot, weight_out, (((1,), (1,)), ((), ())), preferred_element_type=jnp.float32
        )
        * scale_out
    )
    return (up_half, silu_val, slope_val, act_cot, gate_grad, active, out_cot)


def expert_back(up_half, silu_val, slope_val, act_cot, weight_in, scale_in):
    pre_cot = jnp.concatenate([act_cot * up_half * slope_val, act_cot * silu_val], axis=1).astype(
        jnp.bfloat16
    )
    rows_dx = (
        lax.dot_general(
            pre_cot, weight_in, (((1,), (1,)), ((), ())), preferred_element_type=jnp.float32
        )
        * scale_in
    ).astype(jnp.bfloat16)
    return (pre_cot, rows_dx)


def adam_update(weight, first, second, grad, fresh, dead_flag):
    first_new = beta_one * first.astype(jnp.float32) + (1.0 - beta_one) * grad
    second_new = beta_two * second.astype(jnp.float32) + (1.0 - beta_two) * grad * grad
    first_hat = first_new / (1.0 - beta_one**adam_count)
    second_hat = second_new / (1.0 - beta_two**adam_count)
    stepped = weight.astype(jnp.float32) - learn_rate * first_hat / (
        jnp.sqrt(second_hat) + adam_eps
    )
    alive_mask = dead_flag == 0
    return (
        jnp.where(alive_mask, stepped, fresh.astype(jnp.float32)).astype(jnp.bfloat16),
        jnp.where(alive_mask, first_new, jnp.zeros_like(first_new)).astype(jnp.bfloat16),
        jnp.where(alive_mask, second_new, jnp.zeros_like(second_new)).astype(jnp.bfloat16),
    )


def dispatch_match(route_rows, num_exp, capacity):
    flat_routes = route_rows.reshape(-1)
    onehot = (flat_routes[:, None] == jnp.arange(num_exp, dtype=jnp.int32)[None, :]).astype(
        jnp.int32
    )
    slot_rank = jnp.sum((jnp.cumsum(onehot, axis=0) - onehot) * onehot, axis=1)
    target = (flat_routes * capacity + slot_rank).reshape(route_rows.shape)
    return target[None, :, :] == jnp.arange(num_exp * capacity, dtype=jnp.int32)[:, None, None]


def pack_rows(matched, picker, token_rows, cot_rows, gate_rows, num_exp, capacity):
    sent_in = jnp.dot(picker, token_rows, preferred_element_type=jnp.float32).astype(jnp.bfloat16)
    sent_cot = jnp.dot(picker, cot_rows, preferred_element_type=jnp.float32).astype(jnp.bfloat16)
    sent_gate = jnp.sum(
        jnp.where(matched, gate_rows[None, :, :].astype(jnp.float32), 0.0), axis=(1, 2)
    ).astype(jnp.bfloat16)
    return (
        sent_in.reshape(num_exp, capacity, -1),
        sent_cot.reshape(num_exp, capacity, -1),
        sent_gate.reshape(num_exp, capacity),
    )


def body(
    tokens,
    cotangent,
    routes,
    gates,
    collapsed,
    w_in,
    w_out,
    first_in,
    second_in,
    first_out,
    second_out,
    fresh_in,
    fresh_out,
):
    micro_count, tok_rows, model_width = tokens.shape
    route_width = routes.shape[2]
    sources = lax.axis_size("exp")
    num_exp = w_in.shape[0] * sources
    capacity = min(tok_rows, (4 * tok_rows * route_width + 3 * num_exp - 1) // (3 * num_exp))
    full_in, full_out = (
        lax.all_gather(w_in, "rep", axis=1, tiled=True),
        lax.all_gather(w_out, "rep", axis=1, tiled=True),
    )
    weight_in = full_in[0]
    weight_out = full_out[0]
    hidden = weight_out.shape[0]
    scale_in = 1.0 / math.sqrt(model_width)
    scale_out = 1.0 / math.sqrt(hidden)
    matches = [
        dispatch_match(routes[which_micro], num_exp, capacity) for which_micro in range(micro_count)
    ]
    pickers = [jnp.any(matched, axis=2).astype(jnp.bfloat16) for matched in matches]
    packs = [
        pack_rows(
            matches[which_micro],
            pickers[which_micro],
            tokens[which_micro],
            cotangent[which_micro],
            gates[which_micro],
            num_exp,
            capacity,
        )
        for which_micro in range(micro_count)
    ]
    joined = [jnp.concatenate([packed[member] for packed in packs], axis=1) for member in range(3)]
    arrived = (
        lax.all_to_all(joined[0], "exp", split_axis=0, concat_axis=0, tiled=True),
        lax.all_to_all(joined[1], "exp", split_axis=0, concat_axis=0, tiled=True),
        lax.all_to_all(joined[2], "exp", split_axis=0, concat_axis=0, tiled=True),
    )
    rows_in = arrived[0].reshape(-1, model_width)
    rows_cot = arrived[1].reshape(-1, model_width)
    rows_gate = arrived[2].reshape(-1)
    front_vals = expert_front(
        rows_in, rows_cot, rows_gate, weight_in, weight_out, scale_in, scale_out
    )
    grad_out = (
        lax.dot_general(
            front_vals[5],
            front_vals[6],
            (((0,), (0,)), ((), ())),
            preferred_element_type=jnp.float32,
        )
        * scale_out
    )
    fronts = (rows_in, front_vals)
    rows_in, front_vals = fronts
    pre_cot, rows_dx = expert_back(
        front_vals[0], front_vals[1], front_vals[2], front_vals[3], weight_in, scale_in
    )
    grad_in = (
        lax.dot_general(
            rows_in, pre_cot, (((0,), (0,)), ((), ())), preferred_element_type=jnp.float32
        )
        * scale_in
    )
    back_vals = (rows_dx, front_vals[4].astype(jnp.bfloat16))
    summed_in, summed_out = (
        lax.psum_scatter(
            grad_in[None].astype(jnp.bfloat16), "rep", scatter_dimension=1, tiled=True
        ).astype(jnp.float32),
        lax.psum_scatter(
            grad_out[None].astype(jnp.bfloat16), "rep", scatter_dimension=1, tiled=True
        ).astype(jnp.float32),
    )
    rows_dx, gate_grad = back_vals
    returned = (
        lax.all_to_all(
            rows_dx.reshape(sources, -1, model_width),
            "exp",
            split_axis=0,
            concat_axis=0,
            tiled=True,
        ),
        lax.all_to_all(
            gate_grad.reshape(sources, -1), "exp", split_axis=0, concat_axis=0, tiled=True
        ),
    )
    parts_dx = returned[0].reshape(num_exp, micro_count, capacity, model_width)
    parts_gate = returned[1].reshape(num_exp, micro_count, capacity)
    results = [
        (parts_dx[:, which_micro].reshape(-1, model_width), parts_gate[:, which_micro].reshape(-1))
        for which_micro in range(micro_count)
    ]
    token_dx = []
    token_gate = []
    for which_micro in range(micro_count):
        token_dx.append(
            lax.dot_general(
                pickers[which_micro],
                results[which_micro][0],
                (((0,), (0,)), ((), ())),
                preferred_element_type=jnp.float32,
            ).astype(jnp.bfloat16)
        )
        token_gate.append(
            jnp.sum(
                jnp.where(
                    matches[which_micro],
                    results[which_micro][1].astype(jnp.float32)[:, None, None],
                    0.0,
                ),
                axis=0,
            ).astype(jnp.bfloat16)
        )
    dead_flag = collapsed.reshape(-1, 1, 1)
    updated_in = adam_update(w_in, first_in, second_in, summed_in, fresh_in, dead_flag)
    updated_out = adam_update(w_out, first_out, second_out, summed_out, fresh_out, dead_flag)
    return (
        jnp.stack(token_dx),
        jnp.stack(token_gate),
        updated_in[0],
        updated_out[0],
        updated_in[1],
        updated_in[2],
        updated_out[1],
        updated_out[2],
    )


MESH = pl.DeviceIdType.MESH
Z_SIDE = 4


def where_am_i():
    y = lax.axis_index("rep")
    e = lax.axis_index("exp")
    return y, e // 4, (e // 2) % 2, e % 2


def place_of(here, dy, dz, dx, dc):
    y, z, x, c = here
    return (y + dy) % 2, ((z + dz) % Z_SIDE) * 4 + ((x + dx) % 2) * 2 + (c + dc) % 2


def slot_of(here, dy, dz, dx, dc):
    rep, exp = place_of(here, dy, dz, dx, dc)
    return rep * 16 + exp


def greet(here):
    barrier = pltpu.get_barrier_semaphore()
    near = [(1, 0, 0, 0), (0, 1, 0, 0), (0, 2, 0, 0), (0, 3, 0, 0), (0, 0, 1, 0), (0, 0, 0, 1)]
    for step in near:
        pl.semaphore_signal(barrier, inc=1, device_id=place_of(here, *step), device_id_type=MESH)
    pl.semaphore_wait(barrier, len(near))


def number_of(rel):
    dy, dz, dx, dc = rel
    return dy * 16 + dz * 4 + dx * 2 + dc


def spread_kernel(
    tok_ref, cot_ref, gate_ref, w_ref, tok_all, cot_all, gate_all, w_all, send, recv, local, w_send, w_recv
):
    here = where_am_i()
    y = here[0]
    own = (0, 0, 0, 0)
    ins = (tok_ref, cot_ref, gate_ref)
    outs = (tok_all, cot_all, gate_all)
    depth = w_ref.shape[1]
    part = w_all.shape[1] // 2

    def copy(kind, rel, target, arrives):
        slot = slot_of(here, *rel)
        source = ins[kind] if rel == own else outs[kind].at[slot]
        return pltpu.make_async_remote_copy(
            src_ref=source,
            dst_ref=outs[kind].at[slot],
            send_sem=send.at[kind, number_of(arrives)],
            recv_sem=recv.at[kind, number_of(arrives)],
            device_id=place_of(here, *target),
            device_id_type=MESH,
        )

    sent = []

    def pass_on(rel, kinds=(0, 1, 2)):
        dy, dz, dx, dc = rel
        for kind in kinds:
            goes = []
            if dx == 0:
                goes.append(((0, 0, 1, 0), (dy, dz, 1, 0)))
            if dx == 0 and dy == 0 and (kind != 1 or dz == 0):
                goes.append(((1, 0, 0, 0), (1, dz, 0, 0)))
            if rel == own or (kind == 1 and dx == 0 and dz == 0):
                for step in (1, 3, 2):
                    goes.append(((0, Z_SIDE - step, 0, 0), (dy, step, 0, 0)))
            goes.append(((0, 0, 0, 1), (dy, dz, dx, 1)))
            for target, arrives in goes:
                one = copy(kind, rel, target, arrives)
                one.start()
                sent.append(one)

    def landed(kind, rel):
        slot = slot_of(here, *rel)
        pltpu.make_async_remote_copy(
            src_ref=outs[kind].at[slot],
            dst_ref=outs[kind].at[slot],
            send_sem=send.at[kind, number_of(rel)],
            recv_sem=recv.at[kind, number_of(rel)],
            device_id=place_of(here, 0, 0, 0, 1),
            device_id_type=MESH,
        ).wait_recv()

    locals_ = []
    for kind in range(3):
        locals_.append(
            pltpu.make_async_copy(ins[kind], outs[kind].at[slot_of(here, *own)], local.at[kind])
        )
    rows = pl.ds(pl.multiple_of(y * depth, depth), depth)
    for side in range(2):
        locals_.append(
            pltpu.make_async_copy(
                w_ref.at[0, :, pl.ds(pl.multiple_of(side * 2 * part + y * part, 128), part)],
                w_all.at[rows, pl.ds(side * part, part)],
                local.at[3 + side],
            )
        )
    for one in locals_:
        one.start()
    greet(here)
    pass_on(own)
    swaps = []
    for side in range(2):
        swaps.append(
            pltpu.make_async_remote_copy(
                src_ref=w_ref.at[
                    0, :, pl.ds(pl.multiple_of(side * 2 * part + (1 - y) * part, 128), part)
                ],
                dst_ref=w_all.at[rows, pl.ds(side * part, part)],
                send_sem=w_send.at[side],
                recv_sem=w_recv.at[side],
                device_id=place_of(here, 1, 0, 0, 0),
                device_id_type=MESH,
            )
        )
    order = [(1, 0, 0, 0), (0, 1, 0, 0), (0, 3, 0, 0), (0, 0, 1, 0), (1, 1, 0, 0), (1, 3, 0, 0)]
    order += [(0, 2, 0, 0), (1, 0, 1, 0), (1, 2, 0, 0)]
    for dz in (1, 3, 2):
        for dy in (0, 1):
            order.append((dy, dz, 1, 0))
    for rel in order:
        for kind in range(3):
            landed(kind, rel)
            pass_on(rel, (kind,))
        if rel == order[0]:
            for one in swaps:
                one.start()
    for dy in range(2):
        for dz in range(Z_SIDE):
            for dx in range(2):
                for kind in range(3):
                    landed(kind, (dy, dz, dx, 1))
    for one in sent:
        one.wait_send()
    for one in swaps:
        one.wait()
    for one in locals_:
        one.wait()


def spread_all(tok, cot, gate, w_in):
    rows, width = tok.shape
    depth, columns = w_in.shape[1:]
    whole = pl.BlockSpec(memory_space=pl.ANY)
    return pl.pallas_call(
        spread_kernel,
        out_shape=(
            jax.ShapeDtypeStruct((32, rows, width), jnp.bfloat16),
            jax.ShapeDtypeStruct((32, rows, width), jnp.bfloat16),
            jax.ShapeDtypeStruct((32,) + gate.shape, gate.dtype),
            jax.ShapeDtypeStruct((2 * depth, columns // 2), jnp.bfloat16),
        ),
        in_specs=[whole] * 4,
        out_specs=(whole,) * 4,
        scratch_shapes=[
            pltpu.SemaphoreType.DMA((3, 32)),
            pltpu.SemaphoreType.DMA((3, 32)),
            pltpu.SemaphoreType.DMA((5,)),
            pltpu.SemaphoreType.DMA((2,)),
            pltpu.SemaphoreType.DMA((2,)),
        ],
        compiler_params=pltpu.CompilerParams(collective_id=0, has_side_effects=True),
        name="spread_all",
    )(tok, cot, gate, w_in)


def merge_kernel(
    dx_ref,
    dg_ref,
    grad_ref,
    dx_out,
    dg_out,
    grad_out,
    r1x,
    r2x,
    r3x,
    r4x,
    s2x,
    s3x,
    s4x,
    r1g,
    r2g,
    r3g,
    r4g,
    s2g,
    s3g,
    s4g,
    send,
    recv,
    local,
    g_send,
    g_recv,
):
    here = where_am_i()
    y = here[0]
    depth = grad_out.shape[0]
    part = grad_ref.shape[1] // 2
    ins = (dx_ref, dg_ref)
    stage_in = ((r1x, r2x, r3x, r4x), (r1g, r2g, r3g, r4g))
    stage_out = ((None, s2x, s3x, s4x), (None, s2g, s3g, s4g))
    firsts = (0, 16, 24, 30)

    def copy(kind, stage, index, source, target):
        return pltpu.make_async_remote_copy(
            src_ref=source,
            dst_ref=stage_in[kind][stage].at[index],
            send_sem=send.at[kind, firsts[stage] + index],
            recv_sem=recv.at[kind, firsts[stage] + index],
            device_id=place_of(here, *target),
            device_id_type=MESH,
        )

    sent = []

    def go(kind, stage, index, source, target):
        one = copy(kind, stage, index, source, target)
        one.start()
        sent.append(one)

    def landed(kind, stage, index):
        buffer = stage_in[kind][stage].at[index]
        copy(kind, stage, index, buffer, (0, 0, 0, 1)).wait_recv()

    def total(kind, rel, depth_of):
        dy, dz, dx, _ = rel
        value = ins[kind][slot_of(here, *rel)].astype(jnp.float32)
        value = value + stage_in[kind][0][dy * 8 + dz * 2 + dx].astype(jnp.float32)
        if depth_of >= 2:
            value = value + stage_in[kind][1][dy * 4 + dz].astype(jnp.float32)
        if depth_of >= 3:
            for index in range(3):
                value = value + stage_in[kind][2][dy * 3 + index].astype(jnp.float32)
        return value

    columns = [pl.ds(pl.multiple_of(side * 2 * part + y * part, 128), part) for side in range(2)]
    near = pl.ds(pl.multiple_of(y * depth, depth), depth)
    far = pl.ds(pl.multiple_of((1 - y) * depth, depth), depth)
    locals_ = [
        pltpu.make_async_copy(
            grad_ref.at[near, pl.ds(side * part, part)],
            grad_out.at[:, columns[side]],
            local.at[side],
        )
        for side in range(2)
    ]
    for one in locals_:
        one.start()
    greet(here)
    turns = ((1, 2), (1, 1), (1, 3), (0, 2), (0, 1), (0, 3), (1, 0), (0, 0))
    for dx in (1, 0):
        for dy, dz in turns:
            for kind in range(2):
                source = ins[kind].at[slot_of(here, dy, dz, dx, 1)]
                go(kind, 0, dy * 8 + dz * 2 + dx, source, (0, 0, 0, 1))
    swaps = []
    for side in range(2):
        swaps.append(
            pltpu.make_async_remote_copy(
                src_ref=grad_ref.at[far, pl.ds(side * part, part)],
                dst_ref=grad_out.at[:, columns[side]],
                send_sem=g_send.at[side],
                recv_sem=g_recv.at[side],
                device_id=place_of(here, 1, 0, 0, 0),
                device_id_type=MESH,
            )
        )
        swaps[-1].start()
    for dy, dz in turns:
        for kind in range(2):
            landed(kind, 0, dy * 8 + dz * 2 + 1)
            out = stage_out[kind][1]
            out[dy * 4 + dz] = total(kind, (dy, dz, 1, 0), 1).astype(out.dtype)
            go(kind, 1, dy * 4 + dz, out.at[dy * 4 + dz], (0, 0, 1, 0))
    for dy, dz in turns:
        for kind in range(2):
            landed(kind, 0, dy * 8 + dz * 2)
            landed(kind, 1, dy * 4 + dz)
            if dz:
                index = dy * 3 + dz - 1
                out = stage_out[kind][2]
                out[index] = total(kind, (dy, dz, 0, 0), 2).astype(out.dtype)
                go(kind, 2, index, out.at[index], (0, dz, 0, 0))
    for kind in range(2):
        for index in range(3):
            landed(kind, 2, 3 + index)
        out = stage_out[kind][3]
        out[0] = total(kind, (1, 0, 0, 0), 3).astype(out.dtype)
        go(kind, 3, 0, out.at[0], (1, 0, 0, 0))
    for kind in range(2):
        for index in range(3):
            landed(kind, 2, index)
        value = total(kind, (0, 0, 0, 0), 3)
        landed(kind, 3, 0)
        value = value + stage_in[kind][3][0].astype(jnp.float32)
        result = (dx_out, dg_out)[kind]
        result[...] = value.astype(result.dtype)
    for one in sent:
        one.wait_send()
    for one in swaps:
        one.wait()
    for one in locals_:
        one.wait()


def merge_all(dx, dg, grad):
    rows, width = dx.shape[1:]
    depth, columns = grad.shape
    vmem = pl.BlockSpec(memory_space=pltpu.VMEM)
    whole = pl.BlockSpec(memory_space=pl.ANY)
    wide = [pltpu.VMEM((n, rows, width), jnp.bfloat16) for n in (16, 8, 6, 1, 8, 6, 1)]
    small = [pltpu.VMEM((n,) + dg.shape[1:], jnp.float32) for n in (16, 8, 6, 1, 8, 6, 1)]
    return pl.pallas_call(
        merge_kernel,
        out_shape=(
            jax.ShapeDtypeStruct((rows, width), jnp.bfloat16),
            jax.ShapeDtypeStruct(dg.shape[1:], jnp.float32),
            jax.ShapeDtypeStruct((depth // 2, 2 * columns), jnp.bfloat16),
        ),
        in_specs=[vmem, vmem, whole],
        out_specs=(vmem, vmem, whole),
        scratch_shapes=wide
        + small
        + [
            pltpu.SemaphoreType.DMA((2, 31)),
            pltpu.SemaphoreType.DMA((2, 31)),
            pltpu.SemaphoreType.DMA((2,)),
            pltpu.SemaphoreType.DMA((2,)),
            pltpu.SemaphoreType.DMA((2,)),
        ],
        compiler_params=pltpu.CompilerParams(
            collective_id=1, has_side_effects=True, vmem_limit_bytes=40 * 1024 * 1024
        ),
        name="merge_all",
    )(dx, dg, grad)


def partial_body(
    tokens,
    cotangent,
    routes,
    gates,
    collapsed,
    w_in,
    w_out,
    first_in,
    second_in,
    first_out,
    second_out,
    fresh_in,
    fresh_out,
):
    micro, rows, width = tokens.shape
    num_exp = lax.axis_size("exp")
    hidden = w_in.shape[2] // 2
    part = hidden // lax.axis_size("rep")
    me_exp = lax.axis_index("exp")
    scale_in = 1.0 / math.sqrt(width)
    scale_out = 1.0 / math.sqrt(hidden)
    weight_out = w_out[0]
    own_rows = micro * rows
    lanes = 128

    chosen = routes.reshape(own_rows, -1, 1) == jnp.arange(num_exp, dtype=jnp.int32)
    held_gates = gates.reshape(own_rows, -1, 1).astype(jnp.float32)
    spread = jnp.sum(jnp.where(chosen, held_gates, 0.0), axis=1).T
    spread = jnp.pad(spread, ((0, 0), (0, lanes - own_rows))).astype(jnp.bfloat16)
    all_tokens, all_cots, all_gates, weight_in = spread_all(
        tokens.reshape(own_rows, width), cotangent.reshape(own_rows, width), spread, w_in
    )
    all_tokens = all_tokens.reshape(-1, width)
    all_cots = all_cots.reshape(-1, width)
    gate = lax.dynamic_index_in_dim(all_gates, me_exp, 1, keepdims=False)[:, :own_rows]
    gate = gate.astype(jnp.float32).reshape(-1, 1)

    pre = jnp.dot(all_tokens, weight_in, preferred_element_type=jnp.float32) * scale_in
    half, up = pre[:, :part], pre[:, part:]
    silu_val, slope = silu_parts(half)
    active = (silu_val * up).astype(jnp.bfloat16)
    back = (
        lax.dot_general(
            all_cots, weight_out, (((1,), (1,)), ((), ())), preferred_element_type=jnp.float32
        )
        * scale_out
    )
    gate_grad = jnp.sum(active.astype(jnp.float32) * back, axis=1)
    act_cot = back * gate
    pre_cot = jnp.concatenate([act_cot * up * slope, act_cot * silu_val], axis=1).astype(
        jnp.bfloat16
    )
    gated = (active.astype(jnp.float32) * gate).astype(jnp.bfloat16)
    grad_in = (
        lax.dot_general(
            all_tokens, pre_cot, (((0,), (0,)), ((), ())), preferred_element_type=jnp.float32
        )
        * scale_in
    ).astype(jnp.bfloat16)
    rows_dx = (
        lax.dot_general(
            pre_cot, weight_in, (((1,), (1,)), ((), ())), preferred_element_type=jnp.float32
        )
        * scale_in
    ).astype(jnp.bfloat16)
    is_me = jnp.arange(num_exp, dtype=jnp.int32)[:, None] == me_exp
    dense = jnp.pad(gate_grad.reshape(-1, 1, own_rows), ((0, 0), (0, 0), (0, lanes - own_rows)))
    dense = jnp.where(is_me, dense, 0.0)
    token_dx, token_gate, full_grad = merge_all(
        rows_dx.reshape(-1, own_rows, width), dense, grad_in
    )
    token_dx = token_dx.reshape(micro, rows, width)
    token_gate = token_gate[:, :own_rows].T[:, None, :]
    d_gates = jnp.sum(jnp.where(chosen, token_gate, 0.0), axis=2).astype(jnp.bfloat16)
    d_gates = d_gates.reshape(gates.shape)
    grad_out = (
        lax.dot_general(
            gated, all_cots, (((0,), (0,)), ((), ())), preferred_element_type=jnp.float32
        )
        * scale_out
    )[None]
    full_grad = full_grad[None].astype(jnp.float32)
    dead_flag = collapsed.reshape(-1, 1, 1)
    updated_in = adam_update(w_in, first_in, second_in, full_grad, fresh_in, dead_flag)
    updated_out = adam_update(w_out, first_out, second_out, grad_out, fresh_out, dead_flag)
    return (
        token_dx,
        d_gates,
        updated_in[0],
        updated_out[0],
        updated_in[1],
        updated_in[2],
        updated_out[1],
        updated_out[2],
    )


def solution(mesh):
    narrow = mesh.shape["rep"] == 2 and mesh.shape["exp"] == 16
    inner = partial_body if narrow else body
    placed = (
        P(None, ("rep", "exp"), None),
        P(None, ("rep", "exp"), None),
        P(None, ("rep", "exp"), None),
        P(None, ("rep", "exp"), None),
        P("exp"),
        P("exp", "rep", None),
        P("exp", "rep", None),
        P("exp", "rep", None),
        P("exp", "rep", None),
        P("exp", "rep", None),
        P("exp", "rep", None),
        P("exp", "rep", None),
        P("exp", "rep", None),
    )
    return jax.shard_map(
        inner,
        mesh=mesh,
        in_specs=placed,
        out_specs=(
            P(None, ("rep", "exp"), None),
            P(None, ("rep", "exp"), None),
            P("exp", "rep", None),
            P("exp", "rep", None),
            P("exp", "rep", None),
            P("exp", "rep", None),
            P("exp", "rep", None),
            P("exp", "rep", None),
        ),
        check_vma=False,
    )
```
